128 devices in a mesh: ctx: 2 (over y_hi), fsdp: 64 (over y_lo, x, z, core).
Axes of the slice: x: 4, y: 4 (y_hi: 2, y_lo: 2; y = y_hi * 2 + y_lo), z: 4, core: 2. Of those that a mesh axis runs over, the one named last changes fastest.
Arguments:
- layer_in: bfloat16 [64, 256, 2048], P('fsdp', 'ctx'), may hold values from -6 to 6
- segment: int32 [64, 256], P('fsdp'), may hold values from 0 to 4, as said below
- position: int32 [64, 256], P('fsdp'), may hold values from 0 to 159, as said below
- first_gain: bfloat16 [2048], P(('ctx', 'fsdp')), may hold values from 0.5 to 1.5
- first_shift: bfloat16 [2048], P(('ctx', 'fsdp')), may hold values from -1.5 to 1.5
- attend_weight: bfloat16 [2048, 6144], P(('ctx', 'fsdp')), may hold values from -0.125 to 0.125
- attend_bias: bfloat16 [6144], P(('ctx', 'fsdp')), may hold values from -2.5 to 2.5
- output_weight: bfloat16 [2048, 2048], P(('ctx', 'fsdp')), may hold values from -1 to 1
- second_gain: bfloat16 [2048], P(('ctx', 'fsdp')), may hold values from 0.5 to 1.5
- second_shift: bfloat16 [2048], P(('ctx', 'fsdp')), may hold values from -1.5 to 1.5
- gate_weight: bfloat16 [2048, 5632], P(('ctx', 'fsdp')), may hold values from -0.125 to 0.125
- up_weight: bfloat16 [2048, 5632], P(('ctx', 'fsdp')), may hold values from -0.125 to 0.125
- down_weight: bfloat16 [5632, 2048], P(('ctx', 'fsdp')), may hold values from -0.078125 to 0.078125
- cotangent: bfloat16 [64, 256, 2048], P('fsdp', 'ctx'), may hold values from -6 to 6
Outputs:
- layer_out: bfloat16 [64, 256, 2048], P('fsdp', 'ctx')
- input_grad: bfloat16 [64, 256, 2048], P('fsdp', 'ctx')
- first_gain_grad: float32 [2048], P(('ctx', 'fsdp'))
- first_shift_grad: float32 [2048], P(('ctx', 'fsdp'))
- attend_weight_grad: float32 [2048, 6144], P(('ctx', 'fsdp'))
- attend_bias_grad: float32 [6144], P(('ctx', 'fsdp'))
- output_weight_grad: float32 [2048, 2048], P(('ctx', 'fsdp'))
- second_gain_grad: float32 [2048], P(('ctx', 'fsdp'))
- second_shift_grad: float32 [2048], P(('ctx', 'fsdp'))
- gate_weight_grad: float32 [2048, 5632], P(('ctx', 'fsdp'))
- up_weight_grad: float32 [2048, 5632], P(('ctx', 'fsdp'))
- down_weight_grad: float32 [5632, 2048], P(('ctx', 'fsdp'))
The draws below stay inside these ranges and needn't reach their ends.
Inputs may be any that keep to these rules, and one draw needn't show every extreme that they name: Within each group the tokens fall in aligned blocks of 32: segment 0 is the prompt of 128 tokens, segments 1 to 4 are continuations of 32 tokens each, one block each; each index of ctx holds an equal share of the prompt's blocks and of the continuations, in an order drawn from the seed. A prompt token's position is its place in the prompt; a continuation token's is 128 plus its place in its continuation; positions rise by one within a block.
All inputs are finite; a program needn't handle non-finite values.
Results may differ from the reference program's by a relative error of at most 0.015.
Values may be sent and summed in bfloat16 or wider, within the bound.
No kernel may reach another device: no remote copies, remote signals or barrier semaphores. Data moves between devices by JAX's collectives and lax.ppermute only.
A program may use at most 512 MiB of HBM per device.

```python
import math
import jax
import jax.numpy as jnp
from jax import lax

HEADS = 32
HD = 64
D = 2048
FF = 5632
ROT = 16
CONTS = 4
GROUPS = 64
GROUP_ROWS = 256
CONT_LEN = 32
DEV_BLOCKS = 4


def shuffle_blocks(sub_key, blocks):
    return jax.random.permutation(sub_key, blocks)


def group_layout(group_key):
    key_prompt, key_cont, key_shuffle = jax.random.split(group_key, 3)
    devices = 2 * CONTS // DEV_BLOCKS
    share = CONTS // devices
    prompt_order = jax.random.permutation(key_prompt, CONTS).astype(jnp.int32)
    cont_order = jax.random.permutation(key_cont, CONTS).astype(jnp.int32) + CONTS
    per_device = jnp.concatenate([prompt_order.reshape(devices, share), cont_order.reshape(devices, share)], axis=1)
    shuffle_keys = jax.random.split(key_shuffle, devices)
    shuffled = jax.vmap(shuffle_blocks)(shuffle_keys, per_device)
    block_ids = shuffled.reshape(-1)
    offsets = jnp.arange(CONT_LEN, dtype=jnp.int32)
    is_cont = block_ids >= CONTS
    seg_ids = jnp.where(is_cont, block_ids - CONTS + 1, 0).astype(jnp.int32)
    starts = jnp.where(is_cont, CONTS * CONT_LEN, block_ids * CONT_LEN).astype(jnp.int32)
    seg_rows = (seg_ids[:, None] + 0 * offsets[None, :]).reshape(-1)
    pos_rows = (starts[:, None] + offsets[None, :]).reshape(-1)
    return (seg_rows, pos_rows)


def all_layouts(key):
    group_keys = jax.random.split(jax.random.fold_in(key, 4242), GROUPS)
    return jax.vmap(group_layout)(group_keys)


def draw_segment(key, part):
    return all_layouts(key)[0].astype(jnp.int32)


def draw_position(key, part):
    return all_layouts(key)[1].astype(jnp.int32)


def shard_levels(own_key, dims, pieces, smallest, top_value):
    level = 1.0
    for dim, shards_of in pieces:
        heights = jax.random.uniform(jax.random.fold_in(jax.random.fold_in(own_key, 6), dim), (shards_of,), jnp.float32, smallest / len(pieces), top_value / len(pieces))
        level = level * jnp.repeat(jnp.exp(heights), dims[dim] // shards_of).reshape((-1,) + (1,) * (len(dims) - 1 - dim))
    return level


def bell_draw(stream_key, shape, deviation, limit, cuts=(), kind=jnp.bfloat16):
    entries = jax.random.normal(stream_key, shape, jnp.float32) * deviation
    if len(cuts) > 0:
        entries = shard_levels(stream_key, shape, cuts, -0.22, 0.18) * entries
    return jnp.clip(entries, min=-limit, max=limit).astype(kind)


def setup_inputs(seed: int = 0) -> dict:
    streams_of = jax.random.split(jax.random.key(seed), 15)
    layer_in = bell_draw(streams_of[0], (GROUPS, GROUP_ROWS, D), 1.0, 6.0, ((0, 64), (1, 2)))
    segment = draw_segment(jax.random.fold_in(streams_of[14], 71), 0)
    position = draw_position(jax.random.fold_in(streams_of[14], 71), 0)
    first_gain = jnp.clip(1.0 + 0.1 * jax.random.normal(streams_of[3], (D,), jnp.float32), 0.5, 1.5).astype(jnp.bfloat16)
    first_shift = bell_draw(streams_of[4], (D,), 0.3, 1.5, ((0, 128),))
    attend_weight = bell_draw(streams_of[5], (D, 3 * D), D ** -0.5, 0.125, ((0, 128),))
    attend_bias = bell_draw(streams_of[6], (3 * D,), 0.5, 2.5, ((0, 128),))
    output_weight = bell_draw(streams_of[7], (D, D), (D // 64) ** -0.5, 1.0, ((0, 128),))
    second_gain = jnp.clip(1.0 + 0.1 * jax.random.normal(streams_of[8], (D,), jnp.float32), 0.5, 1.5).astype(jnp.bfloat16)
    second_shift = bell_draw(streams_of[9], (D,), 0.3, 1.5, ((0, 128),))
    gate_weight = bell_draw(streams_of[10], (D, FF), D ** -0.5, 0.125, ((0, 128),))
    up_weight = bell_draw(streams_of[11], (D, FF), D ** -0.5, 0.125, ((0, 128),))
    down_weight = bell_draw(streams_of[12], (FF, D), FF ** -0.5, 0.078125, ((0, 128),))
    cotangent = bell_draw(streams_of[13], (GROUPS, GROUP_ROWS, D), 1.0, 6.0, ((0, 64), (1, 2)))
    return {"layer_in": layer_in, "segment": segment, "position": position, "first_gain": first_gain, "first_shift": first_shift, "attend_weight": attend_weight, "attend_bias": attend_bias, "output_weight": output_weight, "second_gain": second_gain, "second_shift": second_shift, "gate_weight": gate_weight, "up_weight": up_weight, "down_weight": down_weight, "cotangent": cotangent}


@jax.custom_vjp
def low(v):
    return lax.optimization_barrier(v.astype(jnp.bfloat16)).astype(jnp.float32)

@jax.custom_vjp
def low_back(v):
    return v

def low_keep(v):
    return (low(v), None)

def low_pass(kept, grad):
    return (grad,)

def back_keep(v):
    return (v, None)

def back_low(kept, grad):
    return (low(grad),)
low.defvjp(low_keep, low_pass)
low_back.defvjp(back_keep, back_low)
HIGHEST = lax.Precision.HIGHEST

def frequencies():
    index = jnp.arange(ROT // 2, dtype=jnp.float32)
    return jnp.exp(index * (-2.0 * math.log(10000.0) / ROT))

def rotate(tensor, cosine, sine):
    half_rot = ROT // 2
    first_part = tensor[..., :half_rot]
    second_part = tensor[..., half_rot:ROT]
    cos_wide = cosine[:, None, :]
    sin_wide = sine[:, None, :]
    return jnp.concatenate([first_part * cos_wide - second_part * sin_wide, second_part * cos_wide + first_part * sin_wide, tensor[..., ROT:]], axis=-1)

def normalize(tok_rows, gain, shift):
    mean_val = lax.optimization_barrier(jnp.mean(tok_rows, axis=-1, keepdims=True))
    centred = tok_rows - mean_val
    variance = lax.optimization_barrier(jnp.mean(centred * centred, axis=-1, keepdims=True))
    return centred * lax.rsqrt(variance + 1e-05) * gain + shift

def attend(inputs):
    queries, keys, values, segment_ids, positions = inputs
    allowed = (positions[None, :] <= positions[:, None]) & ((segment_ids[None, :] == 0) | (segment_ids[None, :] == segment_ids[:, None]))
    scores = low_back(jnp.einsum('qhd,khd->hqk', queries, keys, precision=HIGHEST) * 0.125)
    scores = jnp.where(allowed[None], scores, -1e+30)
    top_val = lax.optimization_barrier(jnp.max(scores, axis=-1, keepdims=True))
    expo = jnp.exp(scores - top_val)
    probs = expo / lax.optimization_barrier(jnp.sum(expo, axis=-1, keepdims=True))
    return jnp.einsum('hqk,khd->qhd', low(probs), values, precision=HIGHEST)

def reference(layer_in, segment, position, first_gain, first_shift, attend_weight, attend_bias, output_weight, second_gain, second_shift, gate_weight, up_weight, down_weight, cotangent):
    groups = layer_in.shape[0]
    group_rows = layer_in.shape[1]
    angles = position.reshape(-1).astype(jnp.float32)[:, None] * frequencies()[None, :]
    cosine = jnp.cos(angles)
    sine = jnp.sin(angles)

    def forward(tokens, gain_one, shift_one, joined_w, joined_b, out_w, gain_two, shift_two, gate_w, up_w, down_w):
        flat = tokens.reshape(-1, D)
        hidden1 = low(normalize(flat, gain_one, shift_one))
        projected = low_back(jnp.dot(hidden1, joined_w, precision=HIGHEST) + joined_b)
        shaped = projected.reshape(-1, 3, HEADS, HD)
        queries = low(rotate(shaped[:, 0], cosine, sine))
        keys = low(rotate(shaped[:, 1], cosine, sine))
        values = low(shaped[:, 2])
        grid_shape = (groups, group_rows, HEADS, HD)
        attended = lax.map(jax.checkpoint(attend), (queries.reshape(grid_shape), keys.reshape(grid_shape), values.reshape(grid_shape), segment, position))
        mixed = low_back(low(attended.reshape(-1, D)))
        resid = flat + low_back(jnp.dot(mixed, out_w, precision=HIGHEST))
        hidden2 = low(normalize(resid, gain_two, shift_two))
        gate_val = low_back(jnp.dot(hidden2, gate_w, precision=HIGHEST))
        up_val = low_back(jnp.dot(hidden2, up_w, precision=HIGHEST))
        product = low(jax.nn.silu(gate_val) * up_val)
        result = resid + jnp.dot(product, down_w, precision=HIGHEST)
        return result.reshape(tokens.shape)
    output, pullback = jax.vjp(forward, layer_in.astype(jnp.float32), first_gain.astype(jnp.float32), first_shift.astype(jnp.float32), attend_weight.astype(jnp.float32), attend_bias.astype(jnp.float32), output_weight.astype(jnp.float32), second_gain.astype(jnp.float32), second_shift.astype(jnp.float32), gate_weight.astype(jnp.float32), up_weight.astype(jnp.float32), down_weight.astype(jnp.float32))
    grads = pullback(cotangent.astype(jnp.float32))
    return (output.astype(jnp.bfloat16), grads[0].astype(jnp.bfloat16), grads[1], grads[2], grads[3], grads[4], grads[5], grads[6], grads[7], grads[8], grads[9], grads[10])
```

```python
import functools
import math

import jax
import jax.numpy as jnp
import numpy as np
from jax import lax
from jax.experimental import pallas as pl
from jax.experimental.pallas import tpu as pltpu
from jax.sharding import Mesh, PartitionSpec as P

HEADS = 32
HD = 64
D = 2048
FF = 5632
ROT = 16
EPS = 1e-05
TOK = 128
NY, NC, NX, NZ = 4, 2, 4, 4
NT = NY * NC
NXZ = NX * NZ
ROWS = D // (NT * NXZ)
FROWS = FF // (NT * NXZ)
FPAD = 48
FT = FPAD * NXZ
HC = D // NT
LH = HC // HD
EXTRA = 128
SIZES = {"yh": 2, "yl": 2, "x": NX, "z": NZ, "c": NC}
AXES = ("yh", "yl", "x", "z", "c")
YC = ("yh", "yl", "c")
XZ = ("x", "z")

f32 = jnp.float32
bf16 = jnp.bfloat16


def shift_perm(axes, deltas):
    sizes = [SIZES[a] for a in axes]
    pairs = []
    for src in range(math.prod(sizes)):
        coord = dict(zip(axes, np.unravel_index(src, sizes)))
        for key, delta in deltas.items():
            if key == "y":
                y = (2 * coord["yh"] + coord["yl"] + delta) % NY
                coord["yh"], coord["yl"] = y // 2, y % 2
            else:
                coord[key] = (coord[key] + delta) % SIZES[key]
        pairs.append((src, int(np.ravel_multi_index([coord[a] for a in axes], sizes))))
    return pairs


def send(value, **deltas):
    axes = tuple(a for a in AXES if a in deltas or (a in ("yh", "yl") and "y" in deltas))
    return lax.ppermute(value, axes, shift_perm(axes, deltas))


class Place:
    def __init__(self):
        yh, yl = lax.axis_index("yh"), lax.axis_index("yl")
        self.c, self.x, self.z = (lax.axis_index(a) for a in ("c", "x", "z"))
        self.y = 2 * yh + yl

    def tensor(self, ry, rc):
        return (self.y + ry) % NY * NC + (self.c ^ rc)

    def row(self, ry, rc):
        y = (self.y + ry) % NY
        return ((y % 2 * NC + (self.c ^ rc)) * 2 + y // 2) * TOK

    def whole(self):
        return ((self.y * NX + self.x) * NZ + self.z) * NC + self.c


EVERY = tuple((r, k) for r in range(NY) for k in range(NC))


def gather_y(own, half):
    from_prev = send(own, y=1)
    from_next = send(own, y=-1)
    top = send(from_prev[:half], y=1)
    bottom = send(from_next[half:], y=-1)
    blocks = {(0, 0): (own,), (1, 0): (from_next,), (3, 0): (from_prev,), (2, 0): (top, bottom)}
    for r in (0, 1, 3, 2):
        blocks[(r, 1)] = tuple(send(b, c=1) for b in blocks[(r, 0)])
    return blocks


def put(blocks, start, shape, axis=0):
    whole = jnp.zeros(shape, bf16)
    for s in EVERY:
        at = 0
        for b in blocks[s]:
            where = [at, 0]
            where[axis] = where[axis] + start(*s)
            whole = lax.dynamic_update_slice(whole, b, tuple(where))
            at += b.shape[0]
    return whole


def gather_rows(own, place):
    return put(gather_y(own, TOK // 2), place.row, (NT * TOK, own.shape[1]))


def reduce_y(total, place):
    part = lambda r, k: lax.dynamic_slice_in_dim(total, place.row(r, k), TOK)
    sums = {}
    half = TOK // 2
    for r in (2, 1, 3, 0):
        other = send(part(r, 1), c=1)
        sums[r] = part(r, 0).astype(f32) + other.astype(f32)
    far = sums[2].astype(bf16)
    top = send(far[:half], y=1)
    bottom = send(far[half:], y=-1)
    one = jnp.concatenate([sums[1][:half] + top.astype(f32), sums[1][half:]], axis=0).astype(bf16)
    three = jnp.concatenate([sums[3][:half], sums[3][half:] + bottom.astype(f32)], axis=0).astype(bf16)
    from_prev = send(one, y=1)
    from_next = send(three, y=-1)
    return sums[0] + from_prev.astype(f32) + from_next.astype(f32)


def all_to_all_y(piece):
    mine = [piece(r, 0) for r in range(NY)]
    other = send(jnp.stack([piece(r, 1) for r in range(NY)]), c=1)
    got = {}
    for r in range(NY):
        pair = jnp.stack([mine[r], other[r]])
        if r:
            pair = send(pair, y=r if r < 3 else -1)
        got[((-r) % NY, 0)] = (pair[0],)
        got[((-r) % NY, 1)] = (pair[1],)
    return got


def to_pi(a):
    n = a.shape[0]
    return a.reshape(n, NY, NXZ, D // NY // NXZ).transpose(0, 2, 1, 3).reshape(n, D)


def from_pi(a):
    n = a.shape[0]
    return a.reshape(n, NXZ, NY, D // NY // NXZ).transpose(0, 2, 1, 3).reshape(n, D)


def norm_stats(rows):
    mean = jnp.mean(rows, axis=-1, keepdims=True)
    centred = rows - mean
    var = jnp.mean(centred * centred, axis=-1, keepdims=True)
    return mean, lax.rsqrt(var + EPS)


def norm_back(grad_h, normed, inv_std, gain):
    grad_n = grad_h * gain
    return inv_std * (
        grad_n
        - jnp.mean(grad_n, axis=-1, keepdims=True)
        - normed * jnp.mean(grad_n * normed, axis=-1, keepdims=True)
    )


GR = 256


def lane_tables(pos):
    lane = lax.broadcasted_iota(jnp.int32, (1, HC), 1) % HD
    index = (lane % (ROT // 2)).astype(f32)
    freq = jnp.exp(index * (-2.0 * math.log(10000.0) / ROT))
    angles = pos * freq
    turned = lane < ROT
    cosine = jnp.where(turned, jnp.cos(angles), 1.0)
    sine = jnp.where(turned, jnp.sin(angles), 0.0)
    return lane < ROT // 2, cosine, sine


def turn(x, first, cosine, sine):
    ahead = pltpu.roll(x, HC - ROT // 2, 1)
    behind = pltpu.roll(x, ROT // 2, 1)
    return x * cosine + jnp.where(first, -ahead, behind) * sine


def dot_t(a, b):
    return lax.dot_general(a, b, (((1,), (1,)), ((), ())), preferred_element_type=f32)


def dot_n(a, b):
    return lax.dot_general(a, b, (((1,), (0,)), ((), ())), preferred_element_type=f32)


def dot_tn(a, b):
    return lax.dot_general(a, b, (((0,), (0,)), ((), ())), preferred_element_type=f32)


def readable(seg_q, pos_q, seg_k, pos_k):
    return (pos_k <= pos_q) & ((seg_k == 0.0) | (seg_k == seg_q))


def softmax_rows(scores):
    top = jnp.max(scores, axis=-1, keepdims=True)
    expo = jnp.exp(scores - top)
    return expo / jnp.sum(expo, axis=-1, keepdims=True)


def attend_kernel(proj_ref, bias_ref, cos_ref, sin_ref, colq_ref, rowk_ref, qkv_ref, mixed_ref):
    lane = lax.broadcasted_iota(jnp.int32, (1, HC), 1)
    first = (lane % HD) < ROT // 2
    cosine, sine = cos_ref[...], sin_ref[...]
    q = turn(proj_ref[:, :HC] + bias_ref[:, :HC], first, cosine, sine).astype(bf16)
    k = turn(proj_ref[:, HC : 2 * HC] + bias_ref[:, HC : 2 * HC], first, cosine, sine).astype(bf16)
    v = (proj_ref[:, 2 * HC :] + bias_ref[:, 2 * HC :]).astype(bf16)
    qkv_ref[:, :HC] = q.astype(f32)
    qkv_ref[:, HC : 2 * HC] = k.astype(f32)
    qkv_ref[:, 2 * HC :] = v.astype(f32)
    allowed = readable(colq_ref[:, 0:1], colq_ref[:, 1:2], rowk_ref[0:1, :], rowk_ref[1:2, :])
    out = jnp.zeros((GR, HC), f32)
    for h in range(LH):
        mine = (lane // HD) == h
        scores = dot_t(jnp.where(mine, q, 0), k) * 0.125
        probs = softmax_rows(jnp.where(allowed, scores, -1e30)).astype(bf16)
        out = jnp.where(mine, dot_n(probs, v), out)
    mixed_ref[...] = out


def attend_back_kernel(qkv_ref, grad_ref, cos_ref, sin_ref, colq_ref, rowk_ref, out_ref, bias_ref):
    lane = lax.broadcasted_iota(jnp.int32, (1, HC), 1)
    first = (lane % HD) < ROT // 2
    cosine, sine = cos_ref[...], sin_ref[...]
    q = qkv_ref[:, :HC].astype(bf16)
    k = qkv_ref[:, HC : 2 * HC].astype(bf16)
    v = qkv_ref[:, 2 * HC :].astype(bf16)
    gm = grad_ref[...].astype(bf16)
    allowed = readable(colq_ref[:, 0:1], colq_ref[:, 1:2], rowk_ref[0:1, :], rowk_ref[1:2, :])
    gq = jnp.zeros((GR, HC), f32)
    gk = jnp.zeros((GR, HC), f32)
    gv = jnp.zeros((GR, HC), f32)
    for h in range(LH):
        mine = (lane // HD) == h
        scores = dot_t(jnp.where(mine, q, 0), k) * 0.125
        probs = softmax_rows(jnp.where(allowed, scores, -1e30))
        gp = dot_t(jnp.where(mine, gm, 0), v)
        gv = jnp.where(mine, dot_tn(probs.astype(bf16), gm), gv)
        row = jnp.sum(probs * gp, axis=-1, keepdims=True)
        gs = (probs * (gp - row)).astype(bf16)
        gq = jnp.where(mine, dot_n(gs, k), gq)
        gk = jnp.where(mine, dot_tn(gs, q), gk)
    gq = turn(gq * 0.125, first, cosine, -sine).astype(bf16)
    gk = turn(gk * 0.125, first, cosine, -sine).astype(bf16)
    gv = gv.astype(bf16)
    out_ref[:, :HC] = gq.astype(f32)
    out_ref[:, HC : 2 * HC] = gk.astype(f32)
    out_ref[:, 2 * HC :] = gv.astype(f32)

    @pl.when(pl.program_id(0) == 0)
    def _():
        bias_ref[...] = jnp.zeros_like(bias_ref)

    for i, g in enumerate((gq, gk, gv)):
        bias_ref[:, i * HC : (i + 1) * HC] += jnp.sum(g.astype(f32), axis=0, keepdims=True)


def group_specs():
    rows = lambda width: pl.BlockSpec((GR, width), lambda g: (g, 0))
    return dict(
        wide=rows(3 * HC),
        narrow=rows(HC),
        cols=rows(2),
        keys=pl.BlockSpec((None, 2, GR), lambda g: (g, 0, 0)),
        bias=pl.BlockSpec((1, 3 * HC), lambda g: (0, 0)),
    )


def attention(projected, bias, cosine, sine, colq, rowk):
    s = group_specs()
    n = projected.shape[0]
    return pl.pallas_call(
        attend_kernel,
        grid=(n // GR,),
        in_specs=[s["wide"], s["bias"], s["narrow"], s["narrow"], s["cols"], s["keys"]],
        out_specs=[s["wide"], s["narrow"]],
        out_shape=[jax.ShapeDtypeStruct((n, 3 * HC), f32), jax.ShapeDtypeStruct((n, HC), f32)],
        compiler_params=pltpu.CompilerParams(vmem_limit_bytes=32 << 20),
        cost_estimate=pl.CostEstimate(flops=4 * n * GR * HC * LH, bytes_accessed=n * HC * 28, transcendentals=n * GR * LH),
        name="attention",
    )(projected, bias, cosine, sine, colq, rowk)


def attention_back(qkv, grad, cosine, sine, colq, rowk):
    s = group_specs()
    n = qkv.shape[0]
    return pl.pallas_call(
        attend_back_kernel,
        grid=(n // GR,),
        in_specs=[s["wide"], s["narrow"], s["narrow"], s["narrow"], s["cols"], s["keys"]],
        out_specs=[s["wide"], s["bias"]],
        out_shape=[jax.ShapeDtypeStruct((n, 3 * HC), f32), jax.ShapeDtypeStruct((1, 3 * HC), f32)],
        compiler_params=pltpu.CompilerParams(vmem_limit_bytes=32 << 20),
        cost_estimate=pl.CostEstimate(flops=10 * n * GR * HC * LH, bytes_accessed=n * HC * 24, transcendentals=n * GR * LH),
        name="attention_back",
    )(qkv, grad, cosine, sine, colq, rowk)


def mm(spec, a, b):
    return jnp.einsum(spec, a, b, preferred_element_type=f32)


def pair_of(own, axis):
    other = send(own, **{axis: 1})
    first = lax.axis_index(axis) == 0
    return jnp.stack([jnp.where(first, own, other), jnp.where(first, other, own)])


def on_device(
    layer_in,
    segment,
    position,
    first_gain,
    first_shift,
    attend_weight,
    attend_bias,
    output_weight,
    second_gain,
    second_shift,
    gate_weight,
    up_weight,
    down_weight,
    cotangent,
):
    place = Place()
    own_row = place.row(0, 0)
    own_rows = lambda a: lax.dynamic_slice_in_dim(a, own_row, TOK)

    joined = attend_weight.reshape(ROWS, 3, NT, HC).transpose(2, 0, 1, 3).reshape(NT, ROWS, 3 * HC)
    small = jnp.concatenate(
        [v.reshape(ROWS, 1) for v in (first_gain, first_shift, second_gain, second_shift)]
        + [attend_bias.reshape(ROWS, 3), jnp.zeros((ROWS, EXTRA - 7), bf16)],
        axis=1,
    )
    joined = jnp.concatenate([joined, jnp.broadcast_to(small[None], (NT, ROWS, EXTRA))], axis=2)
    joined = lax.all_to_all(joined, YC, 0, 0, tiled=True).reshape(NT * ROWS, 3 * HC + EXTRA)
    first_w = lax.all_gather(joined, XZ, axis=0, tiled=True)
    out_w = lax.all_gather(to_pi(output_weight), AXES, axis=0, tiled=True)

    tokens = gather_rows(to_pi(layer_in[0]), place)
    here = jnp.concatenate([segment, position], axis=0).astype(f32)
    rowk = pair_of(here, "yl")
    rowk = pair_of(rowk, "c").transpose(1, 0, 2, 3).reshape(4, 2, GR)
    colq = rowk.transpose(0, 2, 1).reshape(NT * TOK, 2)
    _, cosine, sine = lane_tables(colq[:, 1:2])

    def hidden_cols(w):
        w = w.reshape(ROWS, NY, NXZ, NC, FROWS)
        w = jnp.pad(w, ((0, 0),) * 4 + ((0, FPAD - FROWS),))
        return w.transpose(1, 3, 0, 2, 4).reshape(NT, ROWS, FT)

    gate_up = jnp.concatenate([hidden_cols(gate_weight), hidden_cols(up_weight)], axis=2)
    gate_up = lax.all_to_all(gate_up, YC, 0, 0, tiled=True).reshape(NT * ROWS, 2 * FT)
    down_own = jnp.pad(to_pi(down_weight), ((0, FPAD - FROWS), (0, 0)))

    def pack_down(a):
        rest = jnp.concatenate([a[..., 16 * i : 16 * i + 16, 2 * FT :] for i in range(3)], axis=-1)
        return jnp.concatenate([a[..., : 2 * FT], rest], axis=-2)

    def unpack_down(a):
        w = D - 2 * FT
        rest = jnp.concatenate([a[..., FPAD:, w * i : w * i + w] for i in range(3)], axis=-2)
        return jnp.concatenate([a[..., :FPAD, :], rest], axis=-1)

    second_w = lax.all_gather(jnp.concatenate([gate_up, pack_down(down_own)], axis=0), XZ, axis=0)
    gate_up_w = second_w[:, : NT * ROWS].reshape(D, 2 * FT)
    down_w = unpack_down(second_w[:, NT * ROWS :]).reshape(FT, D)

    joined_w = first_w[:, : 3 * HC]
    small_all = first_w[:, 3 * HC : 3 * HC + 8]
    vectors = small_all[:, :4].astype(f32).T
    gain_one, shift_one, gain_two, shift_two = (vectors[i : i + 1] for i in range(4))
    bias_all = small_all[:, 4:7].reshape(NXZ, NY, NC * ROWS * 3).transpose(1, 0, 2).reshape(3, NT, HC)
    bias = lax.dynamic_index_in_dim(bias_all, place.tensor(0, 0), axis=1, keepdims=False)
    bias = bias.reshape(1, 3 * HC).astype(f32)

    tokens_f = tokens.astype(f32)
    mean_one, inv_one = norm_stats(tokens_f)
    hidden1 = ((tokens_f - mean_one) * inv_one * gain_one + shift_one).astype(bf16)
    projected = mm("td,de->te", hidden1, joined_w)
    qkv, mixed = attention(projected, bias, cosine, sine, colq, rowk)
    mixed = mixed.astype(bf16)
    mixed_all = put(gather_y(mixed, NT * TOK // 2), lambda r, k: place.tensor(r, k) * HC, (NT * TOK, D), axis=1)
    resid = tokens_f + mm("td,de->te", mixed_all, out_w)

    mean_two, inv_two = norm_stats(resid)
    normed2 = (resid - mean_two) * inv_two
    hidden2 = (normed2 * gain_two + shift_two).astype(bf16)
    gate_up_val = mm("td,de->te", hidden2, gate_up_w)
    gate_val, up_val = gate_up_val[:, :FT], gate_up_val[:, FT:]
    sig = jax.nn.sigmoid(gate_val)
    activated = gate_val * sig
    product = (activated * up_val).astype(bf16)
    out_part = mm("tf,fd->td", product, down_w).astype(bf16)
    layer_out = from_pi((own_rows(resid) + reduce_y(out_part, place)).astype(bf16))[None]

    cot = to_pi(cotangent[0])
    grad_top = gather_rows(cot, place)
    grad_prod = mm("td,fd->tf", grad_top, down_w)
    grad_gate = (grad_prod * up_val * sig * (1.0 + gate_val * (1.0 - sig))).astype(bf16)
    grad_up = (grad_prod * activated).astype(bf16)
    grad_gu = jnp.concatenate([grad_gate, grad_up], axis=1)
    h2_part = mm("tf,df->td", grad_gu, gate_up_w)
    gain_two_part = jnp.sum(h2_part * normed2, axis=0)
    shift_two_part = jnp.sum(h2_part, axis=0)
    grad_h2 = reduce_y(h2_part.astype(bf16), place)
    grad_resid = cot.astype(f32) + norm_back(grad_h2, own_rows(normed2), own_rows(inv_two), gain_two)

    down_grad = mm("tf,td->fd", product, grad_top)
    gate_up_grad = mm("td,tf->df", hidden2, grad_gu)
    lane = lax.broadcasted_iota(jnp.int32, (1, 2 * FT), 1)
    gate_up_grad = gate_up_grad + (
        jnp.where(lane == FROWS, gain_two_part[:, None], 0.0) + jnp.where(lane == FROWS + 1, shift_two_part[:, None], 0.0)
    )
    second_chunks = jnp.concatenate(
        [gate_up_grad.astype(bf16).reshape(NXZ, NT * ROWS, 2 * FT), pack_down(down_grad.astype(bf16).reshape(NXZ, FPAD, D))],
        axis=1,
    )
    second_sum = lax.psum_scatter(second_chunks.reshape(-1, 2 * FT), XZ, scatter_dimension=0, tiled=True)
    down_sum = from_pi(unpack_down(second_sum[NT * ROWS :])[:FROWS].astype(f32))
    gate_up_sum = second_sum[: NT * ROWS].reshape(NT, ROWS, 2 * FT)
    gate_up_sum = lax.all_to_all(gate_up_sum, YC, 0, 0, tiled=True).astype(f32)
    gain_two_grad = jnp.sum(gate_up_sum[:, :, FROWS], axis=0)
    shift_two_grad = jnp.sum(gate_up_sum[:, :, FROWS + 1], axis=0)

    def weight_cols(a):
        a = a.reshape(NY, NC, ROWS, NXZ, FPAD)[..., :FROWS]
        return a.transpose(2, 0, 3, 1, 4).reshape(ROWS, FF)

    gate_sum = weight_cols(gate_up_sum[:, :, :FT])
    up_sum = weight_cols(gate_up_sum[:, :, FT:])

    grad_branch = grad_resid.astype(bf16)
    grad_mixed_own = mm("te,de->td", grad_branch, out_w).astype(bf16)
    got = all_to_all_y(lambda r, k: lax.dynamic_slice_in_dim(grad_mixed_own, place.tensor(r, k) * HC, HC, axis=1))
    grad_mixed = put(got, place.row, (NT * TOK, HC))
    grad_proj, bias_part = attention_back(qkv, grad_mixed.astype(f32), cosine, sine, colq, rowk)
    grad_proj = grad_proj.astype(bf16)
    h1_part = mm("te,de->td", grad_proj, joined_w)
    normed1 = (tokens_f - mean_one) * inv_one
    gain_one_part = jnp.sum(h1_part * normed1, axis=0)
    shift_one_part = jnp.sum(h1_part, axis=0)
    grad_h1 = reduce_y(h1_part.astype(bf16), place)
    input_grad = grad_resid + norm_back(grad_h1, own_rows(normed1), own_rows(inv_one), gain_one)
    input_grad = from_pi(input_grad.astype(bf16))[None]

    branch_all = gather_rows(grad_branch, place)
    out_grad = mm("td,te->de", mixed, branch_all).astype(bf16).reshape(NXZ, ROWS, D)
    joined_grad = mm("td,te->de", hidden1, grad_proj)
    bias_block = jnp.broadcast_to(bias_part.reshape(1, ROWS, 3 * HC // ROWS), (D // ROWS, ROWS, 3 * HC // ROWS))
    extra = jnp.concatenate(
        [
            gain_one_part[:, None],
            shift_one_part[:, None],
            bias_block.reshape(D, 3 * HC // ROWS),
            jnp.zeros((D, EXTRA - 2 - 3 * HC // ROWS), f32),
        ],
        axis=1,
    )
    joined_chunks = jnp.concatenate([joined_grad, extra], axis=1).astype(bf16).reshape(NXZ, NT * ROWS, 3 * HC + EXTRA)
    out_chunks = out_grad.reshape(NXZ, ROWS, NT, HC).transpose(0, 2, 1, 3).reshape(NXZ, NT * ROWS, HC)
    first_sum = lax.psum_scatter(jnp.concatenate([joined_chunks, out_chunks], axis=2), XZ, scatter_dimension=0)
    out_mine = first_sum[:, 3 * HC + EXTRA :].reshape(NT, ROWS, HC).transpose(1, 0, 2).reshape(ROWS, D)
    pairs = [(xz * NC + cc, (8 * cc + xz // 2) * NC + xz % 2) for xz in range(NXZ) for cc in range(NC)]
    out_sum = from_pi(lax.ppermute(out_mine, ("x", "z", "c"), pairs)).astype(f32)
    joined_sum = first_sum[:, : 3 * HC + EXTRA].reshape(NT, ROWS, 3 * HC + EXTRA)
    joined_sum = lax.all_to_all(joined_sum, YC, 0, 0, tiled=True).astype(f32)
    attend_sum = joined_sum[:, :, : 3 * HC].reshape(NT, ROWS, 3, HC).transpose(1, 2, 0, 3).reshape(ROWS, 3 * D)
    gain_one_grad = jnp.sum(joined_sum[:, :, 3 * HC], axis=0)
    shift_one_grad = jnp.sum(joined_sum[:, :, 3 * HC + 1], axis=0)
    bias_sum = joined_sum[:, :, 3 * HC + 2 : 3 * HC + 2 + 3 * HC // ROWS].reshape(NT, 3, HC)
    bias_sum = bias_sum.transpose(1, 0, 2).reshape(3 * D)
    bias_grad = lax.dynamic_slice_in_dim(bias_sum, place.whole() * (3 * D // 128), 3 * D // 128)

    return (
        layer_out,
        input_grad,
        gain_one_grad,
        shift_one_grad,
        attend_sum,
        bias_grad,
        out_sum,
        gain_two_grad,
        shift_two_grad,
        gate_sum,
        up_sum,
        down_sum,
    )


def solution(mesh):
    fine = Mesh(np.asarray(mesh.devices).reshape([SIZES[a] for a in AXES]), AXES)
    group, every = ("yl", "x", "z", "c"), AXES
    tokens, whole = P(group, "yh", None), P(every)
    rows = P(every, None)
    return jax.shard_map(
        on_device,
        mesh=fine,
        in_specs=(
            tokens,
            P(group, None),
            P(group, None),
            whole,
            whole,
            rows,
            whole,
            rows,
            whole,
            whole,
            rows,
            rows,
            rows,
            tokens,
        ),
        out_specs=(tokens, tokens, whole, whole, rows, whole, rows, whole, whole, rows, rows, rows),
        check_vma=False,
    )
```

```python
import functools
import math

import jax
import jax.numpy as jnp
import numpy as np
from jax import lax
from jax.experimental import pallas as pl
from jax.experimental.pallas import tpu as pltpu
from jax.experimental.layout import Layout, with_layout_constraint
from jax.sharding import Mesh, PartitionSpec as P

HEADS = 32
HD = 64
D = 2048
FF = 5632
ROT = 16
EPS = 1e-05
TOK = 128
NY, NC, NX, NZ = 4, 2, 4, 4
NT = NY * NC
NXZ = NX * NZ
ROWS = D // (NT * NXZ)
FROWS = FF // (NT * NXZ)
FPAD = 48
FT = FPAD * NXZ
HC = D // NT
LH = HC // HD
EXTRA = 128
SIZES = {"yh": 2, "yl": 2, "x": NX, "z": NZ, "c": NC}
AXES = ("yh", "yl", "x", "z", "c")
YC = ("yh", "yl", "c")
XZ = ("x", "z")

f32 = jnp.float32
bf16 = jnp.bfloat16


def shift_perm(axes, deltas):
    sizes = [SIZES[a] for a in axes]
    pairs = []
    for src in range(math.prod(sizes)):
        coord = dict(zip(axes, np.unravel_index(src, sizes)))
        for key, delta in deltas.items():
            if key == "y":
                y = (2 * coord["yh"] + coord["yl"] + delta) % NY
                coord["yh"], coord["yl"] = y // 2, y % 2
            else:
                coord[key] = (coord[key] + delta) % SIZES[key]
        pairs.append((src, int(np.ravel_multi_index([coord[a] for a in axes], sizes))))
    return pairs


def plain(value):
    return with_layout_constraint(value, Layout(major_to_minor=tuple(range(value.ndim))))


def send(value, **deltas):
    axes = tuple(a for a in AXES if a in deltas or (a in ("yh", "yl") and "y" in deltas))
    return plain(lax.ppermute(plain(value), axes, shift_perm(axes, deltas)))


class Place:
    def __init__(self):
        yh, yl = lax.axis_index("yh"), lax.axis_index("yl")
        self.c, self.x, self.z = (lax.axis_index(a) for a in ("c", "x", "z"))
        self.y = 2 * yh + yl

    def tensor(self, ry, rc):
        return (self.y + ry) % NY * NC + (self.c ^ rc)

    def block(self, ry, rc):
        y = (self.y + ry) % NY
        return (y % 2 * NC + (self.c ^ rc)) * 2 + y // 2

    def whole(self):
        return ((self.y * NX + self.x) * NZ + self.z) * NC + self.c


EVERY = tuple((r, k) for r in range(NY) for k in range(NC))


def gather_y(own, half, hold):
    from_prev = send(own, y=1)
    from_next = send(own, y=-1)
    from_prev, from_next, hold = lax.optimization_barrier((from_prev, from_next, hold))
    top = send(from_prev[:half], y=1)
    bottom = send(from_next[half:], y=-1)
    blocks = {(0, 0): (own,), (1, 0): (from_next,), (3, 0): (from_prev,), (2, 0): (top, bottom)}
    for r in (0, 1, 3, 2):
        blocks[(r, 1)] = tuple(send(b, c=1) for b in blocks[(r, 0)])
    return blocks, hold


def gather_rows(own, place, hold=()):
    blocks, hold = gather_y(own, TOK // 2, hold)
    whole = jnp.zeros((NT,) + own.shape, own.dtype)
    for s in EVERY:
        at = 0
        for b in blocks[s]:
            whole = lax.dynamic_update_slice(whole, b[None], (place.block(*s), at, 0))
            at += b.shape[0]
    whole = whole.reshape(NT * TOK, own.shape[1])
    return (whole, hold) if hold else whole


def reduce_y(total, place, hold=()):
    total = total.reshape(NT, TOK, D)
    part = lambda r, k: lax.dynamic_index_in_dim(total, place.block(r, k), keepdims=False)
    sums = {}
    half = TOK // 2
    for r in (2, 1, 3, 0):
        other = send(part(r, 1), c=1)
        sums[r] = part(r, 0).astype(f32) + other.astype(f32)
    far, hold = lax.optimization_barrier((sums[2].astype(bf16), hold))
    top = send(far[:half], y=1)
    bottom = send(far[half:], y=-1)
    one = jnp.concatenate([sums[1][:half] + top.astype(f32), sums[1][half:]], axis=0).astype(bf16)
    three = jnp.concatenate([sums[3][:half], sums[3][half:] + bottom.astype(f32)], axis=0).astype(bf16)
    from_prev = send(one, y=1)
    from_next = send(three, y=-1)
    out = sums[0] + from_prev.astype(f32) + from_next.astype(f32)
    return (out, hold) if hold else out


def to_pi(a):
    n = a.shape[0]
    return plain(plain(a).reshape(n, NY, NXZ, D // NY // NXZ).transpose(0, 2, 1, 3).reshape(n, D))


def from_pi(a):
    n = a.shape[0]
    return plain(plain(a).reshape(n, NXZ, NY, D // NY // NXZ).transpose(0, 2, 1, 3).reshape(n, D))


def norm_stats(rows):
    mean = jnp.mean(rows, axis=-1, keepdims=True)
    centred = rows - mean
    var = jnp.mean(centred * centred, axis=-1, keepdims=True)
    return mean, lax.rsqrt(var + EPS)


def norm_back(grad_h, normed, inv_std, gain):
    grad_n = grad_h * gain
    return inv_std * (
        grad_n
        - jnp.mean(grad_n, axis=-1, keepdims=True)
        - normed * jnp.mean(grad_n * normed, axis=-1, keepdims=True)
    )


GR = 256


def lane_tables(pos):
    lane = lax.broadcasted_iota(jnp.int32, (1, HC), 1) % HD
    index = (lane % (ROT // 2)).astype(f32)
    freq = jnp.exp(index * (-2.0 * math.log(10000.0) / ROT))
    angles = pos * freq
    turned = lane < ROT
    cosine = jnp.where(turned, jnp.cos(angles), 1.0)
    sine = jnp.where(turned, jnp.sin(angles), 0.0)
    return lane < ROT // 2, cosine, sine


def turn(x, first, cosine, sine):
    ahead = pltpu.roll(x, HC - ROT // 2, 1)
    behind = pltpu.roll(x, ROT // 2, 1)
    return x * cosine + jnp.where(first, -ahead, behind) * sine


def dot_t(a, b):
    return lax.dot_general(a, b, (((1,), (1,)), ((), ())), preferred_element_type=f32)


def dot_n(a, b):
    return lax.dot_general(a, b, (((1,), (0,)), ((), ())), preferred_element_type=f32)


def dot_tn(a, b):
    return lax.dot_general(a, b, (((0,), (0,)), ((), ())), preferred_element_type=f32)


def readable(seg_q, pos_q, seg_k, pos_k):
    return (pos_k <= pos_q) & ((seg_k == 0.0) | (seg_k == seg_q))


def softmax_rows(scores):
    top = jnp.max(scores, axis=-1, keepdims=True)
    expo = jnp.exp(scores - top)
    return expo / jnp.sum(expo, axis=-1, keepdims=True)


def attend_kernel(proj_ref, bias_ref, cos_ref, sin_ref, colq_ref, rowk_ref, qkv_ref, mixed_ref):
    lane = lax.broadcasted_iota(jnp.int32, (1, HC), 1)
    first = (lane % HD) < ROT // 2
    cosine, sine = cos_ref[...], sin_ref[...]
    q = turn(proj_ref[:, :HC] + bias_ref[:, :HC], first, cosine, sine).astype(bf16)
    k = turn(proj_ref[:, HC : 2 * HC] + bias_ref[:, HC : 2 * HC], first, cosine, sine).astype(bf16)
    v = (proj_ref[:, 2 * HC :] + bias_ref[:, 2 * HC :]).astype(bf16)
    qkv_ref[:, :HC] = q.astype(f32)
    qkv_ref[:, HC : 2 * HC] = k.astype(f32)
    qkv_ref[:, 2 * HC :] = v.astype(f32)
    allowed = readable(colq_ref[:, 0:1], colq_ref[:, 1:2], rowk_ref[0:1, :], rowk_ref[1:2, :])
    out = jnp.zeros((GR, HC), f32)
    for h in range(LH):
        mine = (lane // HD) == h
        scores = dot_t(jnp.where(mine, q, 0), k) * 0.125
        probs = softmax_rows(jnp.where(allowed, scores, -1e30)).astype(bf16)
        out = jnp.where(mine, dot_n(probs, v), out)
    mixed_ref[...] = out


def attend_back_kernel(qkv_ref, grad_ref, cos_ref, sin_ref, colq_ref, rowk_ref, out_ref, bias_ref):
    lane = lax.broadcasted_iota(jnp.int32, (1, HC), 1)
    first = (lane % HD) < ROT // 2
    cosine, sine = cos_ref[...], sin_ref[...]
    q = qkv_ref[:, :HC].astype(bf16)
    k = qkv_ref[:, HC : 2 * HC].astype(bf16)
    v = qkv_ref[:, 2 * HC :].astype(bf16)
    gm = grad_ref[...].astype(bf16)
    allowed = readable(colq_ref[:, 0:1], colq_ref[:, 1:2], rowk_ref[0:1, :], rowk_ref[1:2, :])
    gq = jnp.zeros((GR, HC), f32)
    gk = jnp.zeros((GR, HC), f32)
    gv = jnp.zeros((GR, HC), f32)
    for h in range(LH):
        mine = (lane // HD) == h
        scores = dot_t(jnp.where(mine, q, 0), k) * 0.125
        probs = softmax_rows(jnp.where(allowed, scores, -1e30))
        gp = dot_t(jnp.where(mine, gm, 0), v)
        gv = jnp.where(mine, dot_tn(probs.astype(bf16), gm), gv)
        row = jnp.sum(probs * gp, axis=-1, keepdims=True)
        gs = (probs * (gp - row)).astype(bf16)
        gq = jnp.where(mine, dot_n(gs, k), gq)
        gk = jnp.where(mine, dot_tn(gs, q), gk)
    gq = turn(gq * 0.125, first, cosine, -sine).astype(bf16)
    gk = turn(gk * 0.125, first, cosine, -sine).astype(bf16)
    gv = gv.astype(bf16)
    out_ref[:, :HC] = gq.astype(f32)
    out_ref[:, HC : 2 * HC] = gk.astype(f32)
    out_ref[:, 2 * HC :] = gv.astype(f32)

    @pl.when(pl.program_id(0) == 0)
    def _():
        bias_ref[...] = jnp.zeros_like(bias_ref)

    for i, g in enumerate((gq, gk, gv)):
        bias_ref[:, i * HC : (i + 1) * HC] += jnp.sum(g.astype(f32), axis=0, keepdims=True)


def group_specs():
    rows = lambda width: pl.BlockSpec((GR, width), lambda g: (g, 0))
    return dict(
        wide=rows(3 * HC),
        narrow=rows(HC),
        cols=rows(2),
        keys=pl.BlockSpec((None, 2, GR), lambda g: (g, 0, 0)),
        bias=pl.BlockSpec((1, 3 * HC), lambda g: (0, 0)),
    )


def attention(projected, bias, cosine, sine, colq, rowk):
    s = group_specs()
    n = projected.shape[0]
    return pl.pallas_call(
        attend_kernel,
        grid=(n // GR,),
        in_specs=[s["wide"], s["bias"], s["narrow"], s["narrow"], s["cols"], s["keys"]],
        out_specs=[s["wide"], s["narrow"]],
        out_shape=[jax.ShapeDtypeStruct((n, 3 * HC), f32), jax.ShapeDtypeStruct((n, HC), f32)],
        compiler_params=pltpu.CompilerParams(vmem_limit_bytes=32 << 20),
        cost_estimate=pl.CostEstimate(flops=4 * n * GR * HC * LH, bytes_accessed=n * HC * 28, transcendentals=n * GR * LH),
        name="attention",
    )(projected, bias, cosine, sine, colq, rowk)


def attention_back(qkv, grad, cosine, sine, colq, rowk):
    s = group_specs()
    n = qkv.shape[0]
    return pl.pallas_call(
        attend_back_kernel,
        grid=(n // GR,),
        in_specs=[s["wide"], s["narrow"], s["narrow"], s["narrow"], s["cols"], s["keys"]],
        out_specs=[s["wide"], s["bias"]],
        out_shape=[jax.ShapeDtypeStruct((n, 3 * HC), f32), jax.ShapeDtypeStruct((1, 3 * HC), f32)],
        compiler_params=pltpu.CompilerParams(vmem_limit_bytes=32 << 20),
        cost_estimate=pl.CostEstimate(flops=10 * n * GR * HC * LH, bytes_accessed=n * HC * 24, transcendentals=n * GR * LH),
        name="attention_back",
    )(qkv, grad, cosine, sine, colq, rowk)


def mm(spec, a, b):
    return jnp.einsum(spec, a, b, preferred_element_type=f32)


def pair_of(own, axis):
    other = send(own, **{axis: 1})
    first = lax.axis_index(axis) == 0
    return jnp.stack([jnp.where(first, own, other), jnp.where(first, other, own)])


def on_device(
    layer_in,
    segment,
    position,
    first_gain,
    first_shift,
    attend_weight,
    attend_bias,
    output_weight,
    second_gain,
    second_shift,
    gate_weight,
    up_weight,
    down_weight,
    cotangent,
):
    place = Place()
    own_block = place.block(0, 0)
    own_rows = lambda a: lax.dynamic_index_in_dim(a.reshape((NT, TOK) + a.shape[1:]), own_block, keepdims=False)

    joined = attend_weight.reshape(ROWS, 3, NT, HC).transpose(2, 0, 1, 3).reshape(NT, ROWS, 3 * HC)
    small = jnp.concatenate(
        [v.reshape(ROWS, 1) for v in (first_gain, first_shift, second_gain, second_shift)]
        + [attend_bias.reshape(ROWS, 3), jnp.zeros((ROWS, EXTRA - 7), bf16)],
        axis=1,
    )
    joined = jnp.concatenate([joined, jnp.broadcast_to(small[None], (NT, ROWS, EXTRA))], axis=2)
    joined = lax.all_to_all(joined, YC, 0, 0, tiled=True).reshape(NT * ROWS, 3 * HC + EXTRA)
    pairs = [(xz * NC + cc, (8 * cc + xz // 2) * NC + xz % 2) for xz in range(NXZ) for cc in range(NC)]
    out_own = lax.ppermute(to_pi(output_weight), ("x", "z", "c"), [(b, a) for a, b in pairs])
    out_own = out_own.reshape(ROWS, NT, HC).transpose(1, 0, 2).reshape(NT * ROWS, HC)
    first_own = jnp.concatenate([joined, out_own], axis=1)

    layer_pi = to_pi(layer_in[0])
    tokens = gather_rows(layer_pi, place)
    cot = to_pi(cotangent[0])
    here = jnp.concatenate([segment, position], axis=0).astype(f32)
    rowk = pair_of(here, "yl")
    rowk = pair_of(rowk, "c").transpose(1, 0, 2, 3).reshape(4, 2, GR)
    colq = rowk.transpose(0, 2, 1).reshape(NT * TOK, 2)
    _, cosine, sine = lane_tables(colq[:, 1:2])

    first_w = lax.all_gather(first_own, XZ, axis=0)
    hold = (tokens, gate_weight, up_weight, down_weight)
    tokens, gate_weight, up_weight, down_weight = lax.optimization_barrier(hold)

    spread = np.zeros((NXZ, FROWS, NXZ, FPAD), np.float32)
    for k in range(NXZ):
        spread[k, :, k, :FROWS] = np.eye(FROWS)
    spread = jnp.asarray(spread.reshape(NXZ * FROWS, FT), bf16)

    def hidden_cols(w):
        w = plain(w).reshape(ROWS, NT, NXZ * FROWS).transpose(1, 0, 2)
        return mm("trf,fg->trg", w, spread).astype(bf16)

    gate_up = jnp.concatenate([hidden_cols(gate_weight), hidden_cols(up_weight)], axis=2)
    gate_up = lax.all_to_all(gate_up, YC, 0, 0, tiled=True).reshape(NT * ROWS, 2 * FT)
    down_own = lax.ppermute(plain(down_weight), ("x", "z", "c"), [(b, a) for a, b in pairs])
    down_own = jnp.pad(to_pi(down_own), ((0, FPAD - FROWS), (0, 0)))

    def pack_down(a):
        rest = jnp.concatenate([a[..., 16 * i : 16 * i + 16, 2 * FT :] for i in range(3)], axis=-1)
        return jnp.concatenate([a[..., : 2 * FT], rest], axis=-2)

    def unpack_down(a):
        w = D - 2 * FT
        rest = jnp.concatenate([a[..., FPAD:, w * i : w * i + w] for i in range(3)], axis=-2)
        return jnp.concatenate([a[..., :FPAD, :], rest], axis=-1)

    second_own = jnp.concatenate([gate_up, pack_down(down_own)], axis=0)
    second_w = lax.all_gather(second_own, XZ, axis=0)
    gate_up_w = second_w[:, : NT * ROWS].reshape(D, 2 * FT)
    down_w = unpack_down(second_w[:, NT * ROWS :]).reshape(FT, D)

    cot_later, first_w = lax.optimization_barrier((cot, first_w))
    grad_top = gather_rows(cot_later, place)
    out_w = first_w[:, :, 3 * HC + EXTRA :].reshape(NXZ, NT, ROWS, HC).transpose(0, 2, 1, 3).reshape(HC, D)
    first_w = first_w[:, :, : 3 * HC + EXTRA].reshape(D, 3 * HC + EXTRA)
    joined_w = first_w[:, : 3 * HC]
    small_all = first_w[:, 3 * HC : 3 * HC + 8]
    vectors = small_all[:, :4].astype(f32).T
    gain_one, shift_one, gain_two, shift_two = (vectors[i : i + 1] for i in range(4))
    bias_all = small_all[:, 4:7].reshape(NXZ, NY, NC * ROWS * 3).transpose(1, 0, 2).reshape(3, NT, HC)
    bias = lax.dynamic_index_in_dim(bias_all, place.tensor(0, 0), axis=1, keepdims=False)
    bias = bias.reshape(1, 3 * HC).astype(f32)

    tokens_f = tokens.astype(f32)
    mean_one, inv_one = norm_stats(tokens_f)
    hidden1 = ((tokens_f - mean_one) * inv_one * gain_one + shift_one).astype(bf16)
    projected = mm("td,de->te", hidden1, joined_w)
    qkv, mixed = attention(projected, bias, cosine, sine, colq, rowk)
    mixed = mixed.astype(bf16)
    attended = mm("td,de->te", mixed, out_w).astype(bf16)
    resid = layer_pi.astype(f32) + reduce_y(attended, place)

    mean_two, inv_two = norm_stats(resid)
    normed2 = (resid - mean_two) * inv_two
    hidden2 = (normed2 * gain_two + shift_two).astype(bf16)
    hidden2, (gate_up_w, down_w) = gather_rows(hidden2, place, (gate_up_w, down_w))
    gate_up_val = mm("td,de->te", hidden2, gate_up_w)
    gate_val, up_val = gate_up_val[:, :FT], gate_up_val[:, FT:]
    sig = jax.nn.sigmoid(gate_val)
    activated = gate_val * sig
    product = (activated * up_val).astype(bf16)

    grad_prod = mm("td,fd->tf", grad_top, down_w)
    grad_gate = (grad_prod * up_val * sig * (1.0 + gate_val * (1.0 - sig))).astype(bf16)
    grad_up = (grad_prod * activated).astype(bf16)
    grad_gu = jnp.concatenate([grad_gate, grad_up], axis=1)
    h2_part = mm("tf,df->td", grad_gu, gate_up_w)
    later = (product, grad_top, hidden2, grad_gu)
    grad_h2, (product, grad_top, hidden2, grad_gu) = reduce_y(h2_part.astype(bf16), place, later)

    down_grad = mm("tf,td->fd", product, grad_top)
    gate_up_grad = mm("td,tf->df", hidden2, grad_gu)
    second_chunks = jnp.concatenate(
        [gate_up_grad.astype(bf16).reshape(NXZ, NT * ROWS, 2 * FT), pack_down(down_grad.astype(bf16).reshape(NXZ, FPAD, D))],
        axis=1,
    )
    grad_h2, second_chunks = lax.optimization_barrier((grad_h2, second_chunks))
    gain_two_part = jnp.sum(grad_h2 * normed2, axis=0)
    shift_two_part = jnp.sum(grad_h2, axis=0)
    grad_resid = cot.astype(f32) + norm_back(grad_h2, normed2, inv_two, gain_two)
    second_sum = lax.psum_scatter(second_chunks.reshape(-1, 2 * FT), XZ, scatter_dimension=0, tiled=True)
    grad_branch = grad_resid.astype(bf16)
    branch_all = gather_rows(grad_branch, place)
    grad_mixed = mm("te,de->td", branch_all, out_w)
    grad_proj, bias_part = attention_back(qkv, grad_mixed, cosine, sine, colq, rowk)
    grad_proj = grad_proj.astype(bf16)
    h1_part = mm("te,de->td", grad_proj, joined_w)
    normed1 = (tokens_f - mean_one) * inv_one
    gain_one_part = jnp.sum(h1_part * normed1, axis=0)
    shift_one_part = jnp.sum(h1_part, axis=0)
    later = (hidden1, mixed, branch_all)
    grad_h1, (hidden1, mixed, branch_all) = reduce_y(h1_part.astype(bf16), place, later)
    grad_h1, product = lax.optimization_barrier((grad_h1, product))
    out_part = mm("tf,fd->td", product, down_w).astype(bf16)
    layer_out = from_pi((resid + reduce_y(out_part, place)).astype(bf16))[None]
    input_grad = grad_resid + norm_back(grad_h1, own_rows(normed1), own_rows(inv_one), gain_one)
    input_grad = from_pi(input_grad.astype(bf16))[None]

    out_grad = mm("td,te->de", mixed, branch_all).astype(bf16).reshape(NXZ, ROWS, D)
    joined_grad = mm("td,te->de", hidden1, grad_proj)
    bias_block = jnp.broadcast_to(bias_part.reshape(1, ROWS, 3 * HC // ROWS), (D // ROWS, ROWS, 3 * HC // ROWS))
    extra = jnp.concatenate(
        [
            gain_one_part[:, None],
            shift_one_part[:, None],
            gain_two_part[:, None],
            shift_two_part[:, None],
            bias_block.reshape(D, 3 * HC // ROWS),
            jnp.zeros((D, EXTRA - 4 - 3 * HC // ROWS), f32),
        ],
        axis=1,
    )
    joined_chunks = jnp.concatenate([joined_grad, extra], axis=1).astype(bf16).reshape(NXZ, NT * ROWS, 3 * HC + EXTRA)
    out_chunks = out_grad.reshape(NXZ, ROWS, NT, HC).transpose(0, 2, 1, 3).reshape(NXZ, NT * ROWS, HC)
    first_chunks = jnp.concatenate([joined_chunks, out_chunks], axis=2)
    first_chunks, second_sum = lax.optimization_barrier((first_chunks, second_sum))
    first_sum = lax.psum_scatter(first_chunks, XZ, scatter_dimension=0)
    down_sum = unpack_down(second_sum[NT * ROWS :])[:FROWS]
    down_sum = from_pi(lax.ppermute(plain(down_sum), ("x", "z", "c"), pairs)).astype(f32)
    gate_up_sum = second_sum[: NT * ROWS].reshape(NT, ROWS, 2 * FT)
    gate_up_sum = lax.all_to_all(gate_up_sum, YC, 0, 0, tiled=True)

    def weight_cols(a):
        a = mm("trg,fg->trf", a, spread)
        return a.transpose(1, 0, 2).reshape(ROWS, FF)

    gate_sum = weight_cols(gate_up_sum[:, :, :FT])
    up_sum = weight_cols(gate_up_sum[:, :, FT:])

    out_mine = first_sum[:, 3 * HC + EXTRA :].reshape(NT, ROWS, HC).transpose(1, 0, 2).reshape(ROWS, D)
    out_sum = from_pi(lax.ppermute(out_mine, ("x", "z", "c"), pairs)).astype(f32)
    joined_sum = first_sum[:, : 3 * HC + EXTRA].reshape(NT, ROWS, 3 * HC + EXTRA)
    joined_sum = lax.all_to_all(joined_sum, YC, 0, 0, tiled=True).astype(f32)
    attend_sum = joined_sum[:, :, : 3 * HC].reshape(NT, ROWS, 3, HC).transpose(1, 2, 0, 3).reshape(ROWS, 3 * D)
    summed = jnp.sum(joined_sum[:, :, 3 * HC : 3 * HC + 4], axis=0)
    gain_one_grad, shift_one_grad, gain_two_grad, shift_two_grad = (summed[:, i] for i in range(4))
    bias_sum = joined_sum[:, :, 3 * HC + 4 : 3 * HC + 4 + 3 * HC // ROWS].reshape(NT, 3, HC)
    bias_sum = bias_sum.transpose(1, 0, 2).reshape(3 * D)
    bias_grad = lax.dynamic_slice_in_dim(bias_sum, place.whole() * (3 * D // 128), 3 * D // 128)

    return (
        layer_out,
        input_grad,
        gain_one_grad,
        shift_one_grad,
        attend_sum,
        bias_grad,
        out_sum,
        gain_two_grad,
        shift_two_grad,
        gate_sum,
        up_sum,
        down_sum,
    )


def solution(mesh):
    fine = Mesh(np.asarray(mesh.devices).reshape([SIZES[a] for a in AXES]), AXES)
    group, every = ("yl", "x", "z", "c"), AXES
    tokens, whole = P(group, "yh", None), P(every)
    rows = P(every, None)
    return jax.shard_map(
        on_device,
        mesh=fine,
        in_specs=(
            tokens,
            P(group, None),
            P(group, None),
            whole,
            whole,
            rows,
            whole,
            rows,
            whole,
            whole,
            rows,
            rows,
            rows,
            tokens,
        ),
        out_specs=(tokens, tokens, whole, whole, rows, whole, rows, whole, whole, rows, rows, rows),
        check_vma=False,
    )
```

```python
import functools
import math

import jax
import jax.numpy as jnp
import numpy as np
from jax import lax
from jax.experimental import pallas as pl
from jax.experimental.pallas import tpu as pltpu
from jax.experimental.layout import Layout, with_layout_constraint
from jax.sharding import Mesh, PartitionSpec as P

HEADS = 32
HD = 64
D = 2048
FF = 5632
ROT = 16
EPS = 1e-05
TOK = 128
NY, NC, NX, NZ = 4, 2, 4, 4
NT = NY * NC
NXZ = NX * NZ
ROWS = D // (NT * NXZ)
FROWS = FF // (NT * NXZ)
FPAD = 48
FT = FPAD * NXZ
HC = D // NT
LH = HC // HD
EXTRA = 128
SIZES = {"yh": 2, "yl": 2, "x": NX, "z": NZ, "c": NC}
AXES = ("yh", "yl", "x", "z", "c")
YC = ("yh", "yl", "c")
XZ = ("x", "z")

f32 = jnp.float32
bf16 = jnp.bfloat16


def shift_perm(axes, deltas):
    sizes = [SIZES[a] for a in axes]
    pairs = []
    for src in range(math.prod(sizes)):
        coord = dict(zip(axes, np.unravel_index(src, sizes)))
        for key, delta in deltas.items():
            if key == "y":
                y = (2 * coord["yh"] + coord["yl"] + delta) % NY
                coord["yh"], coord["yl"] = y // 2, y % 2
            else:
                coord[key] = (coord[key] + delta) % SIZES[key]
        pairs.append((src, int(np.ravel_multi_index([coord[a] for a in axes], sizes))))
    return pairs


def plain(value):
    return with_layout_constraint(value, Layout(major_to_minor=tuple(range(value.ndim))))


def send(value, **deltas):
    axes = tuple(a for a in AXES if a in deltas or (a in ("yh", "yl") and "y" in deltas))
    return plain(lax.ppermute(plain(value), axes, shift_perm(axes, deltas)))


class Place:
    def __init__(self):
        yh, yl = lax.axis_index("yh"), lax.axis_index("yl")
        self.c, self.x, self.z = (lax.axis_index(a) for a in ("c", "x", "z"))
        self.y = 2 * yh + yl

    def tensor(self, ry, rc):
        return (self.y + ry) % NY * NC + (self.c ^ rc)

    def block(self, ry, rc):
        y = (self.y + ry) % NY
        return (y % 2 * NC + (self.c ^ rc)) * 2 + y // 2

    def whole(self):
        return ((self.y * NX + self.x) * NZ + self.z) * NC + self.c


EVERY = tuple((r, k) for r in range(NY) for k in range(NC))


def gather_y(own, half, hold, late=None):
    from_prev = send(own, y=1)
    from_next = send(own, y=-1)
    from_prev, from_next, hold = lax.optimization_barrier((from_prev, from_next, hold))
    top = send(from_prev[:half], y=1)
    bottom = send(from_next[half:], y=-1)
    if late:
        top, bottom, hold = lax.optimization_barrier((top, bottom, late(*hold)))
    blocks = {(0, 0): (own,), (1, 0): (from_next,), (3, 0): (from_prev,), (2, 0): (top, bottom)}
    for r in (0, 1, 3, 2):
        blocks[(r, 1)] = tuple(send(b, c=1) for b in blocks[(r, 0)])
    return blocks, hold


def gather_rows(own, place, hold=(), late=None):
    blocks, hold = gather_y(own, TOK // 2, hold, late)
    whole = jnp.zeros((NT,) + own.shape, own.dtype)
    for s in EVERY:
        at = 0
        for b in blocks[s]:
            whole = lax.dynamic_update_slice(whole, b[None], (place.block(*s), at, 0))
            at += b.shape[0]
    whole = whole.reshape(NT * TOK, own.shape[1])
    return (whole, hold) if hold else whole


def reduce_y(total, place, hold=()):
    total = total.reshape(NT, TOK, D)
    part = lambda r, k: lax.dynamic_index_in_dim(total, place.block(r, k), keepdims=False)
    sums = {r: part(r, 0).astype(f32) + send(part(r, 1), c=1).astype(f32) for r in (2, 1, 3, 0)}
    away, hold = lax.optimization_barrier(({r: sums[r].astype(bf16) for r in (2, 1, 3)}, hold))
    out = sums[0]
    for r in (2, 1, 3):
        out = out + send(away[r], y=r).astype(f32)
    return (out, hold) if hold else out


def to_pi(a):
    n = a.shape[0]
    return plain(plain(a).reshape(n, NY, NXZ, D // NY // NXZ).transpose(0, 2, 1, 3).reshape(n, D))


def from_pi(a):
    n = a.shape[0]
    return plain(plain(a).reshape(n, NXZ, NY, D // NY // NXZ).transpose(0, 2, 1, 3).reshape(n, D))


def norm_stats(rows):
    mean = jnp.mean(rows, axis=-1, keepdims=True)
    centred = rows - mean
    var = jnp.mean(centred * centred, axis=-1, keepdims=True)
    return mean, lax.rsqrt(var + EPS)


def norm_back(grad_h, normed, inv_std, gain):
    grad_n = grad_h * gain
    return inv_std * (
        grad_n
        - jnp.mean(grad_n, axis=-1, keepdims=True)
        - normed * jnp.mean(grad_n * normed, axis=-1, keepdims=True)
    )


GR = 256


def lane_tables(pos):
    lane = lax.broadcasted_iota(jnp.int32, (1, HC), 1) % HD
    index = (lane % (ROT // 2)).astype(f32)
    freq = jnp.exp(index * (-2.0 * math.log(10000.0) / ROT))
    angles = pos * freq
    turned = lane < ROT
    cosine = jnp.where(turned, jnp.cos(angles), 1.0)
    sine = jnp.where(turned, jnp.sin(angles), 0.0)
    return lane < ROT // 2, cosine, sine


def turn(x, first, cosine, sine):
    ahead = pltpu.roll(x, HC - ROT // 2, 1)
    behind = pltpu.roll(x, ROT // 2, 1)
    return x * cosine + jnp.where(first, -ahead, behind) * sine


def dot_t(a, b):
    return lax.dot_general(a, b, (((1,), (1,)), ((), ())), preferred_element_type=f32)


def dot_n(a, b):
    return lax.dot_general(a, b, (((1,), (0,)), ((), ())), preferred_element_type=f32)


def dot_tn(a, b):
    return lax.dot_general(a, b, (((0,), (0,)), ((), ())), preferred_element_type=f32)


def readable(seg_q, pos_q, seg_k, pos_k):
    return (pos_k <= pos_q) & ((seg_k == 0.0) | (seg_k == seg_q))


def softmax_rows(scores):
    top = jnp.max(scores, axis=-1, keepdims=True)
    expo = jnp.exp(scores - top)
    return expo / jnp.sum(expo, axis=-1, keepdims=True)


def attend_kernel(proj_ref, bias_ref, cos_ref, sin_ref, colq_ref, rowk_ref, qkv_ref, mixed_ref):
    lane = lax.broadcasted_iota(jnp.int32, (1, HC), 1)
    first = (lane % HD) < ROT // 2
    cosine, sine = cos_ref[...], sin_ref[...]
    q = turn(proj_ref[:, :HC] + bias_ref[:, :HC], first, cosine, sine).astype(bf16)
    k = turn(proj_ref[:, HC : 2 * HC] + bias_ref[:, HC : 2 * HC], first, cosine, sine).astype(bf16)
    v = (proj_ref[:, 2 * HC :] + bias_ref[:, 2 * HC :]).astype(bf16)
    qkv_ref[:, :HC] = q.astype(f32)
    qkv_ref[:, HC : 2 * HC] = k.astype(f32)
    qkv_ref[:, 2 * HC :] = v.astype(f32)
    allowed = readable(colq_ref[:, 0:1], colq_ref[:, 1:2], rowk_ref[0:1, :], rowk_ref[1:2, :])
    out = jnp.zeros((GR, HC), f32)
    for h in range(LH):
        mine = (lane // HD) == h
        scores = dot_t(jnp.where(mine, q, 0), k) * 0.125
        probs = softmax_rows(jnp.where(allowed, scores, -1e30)).astype(bf16)
        out = jnp.where(mine, dot_n(probs, v), out)
    mixed_ref[...] = out


def attend_back_kernel(qkv_ref, grad_ref, cos_ref, sin_ref, colq_ref, rowk_ref, out_ref, bias_ref):
    lane = lax.broadcasted_iota(jnp.int32, (1, HC), 1)
    first = (lane % HD) < ROT // 2
    cosine, sine = cos_ref[...], sin_ref[...]
    q = qkv_ref[:, :HC].astype(bf16)
    k = qkv_ref[:, HC : 2 * HC].astype(bf16)
    v = qkv_ref[:, 2 * HC :].astype(bf16)
    gm = grad_ref[...].astype(bf16)
    allowed = readable(colq_ref[:, 0:1], colq_ref[:, 1:2], rowk_ref[0:1, :], rowk_ref[1:2, :])
    gq = jnp.zeros((GR, HC), f32)
    gk = jnp.zeros((GR, HC), f32)
    gv = jnp.zeros((GR, HC), f32)
    for h in range(LH):
        mine = (lane // HD) == h
        scores = dot_t(jnp.where(mine, q, 0), k) * 0.125
        probs = softmax_rows(jnp.where(allowed, scores, -1e30))
        gp = dot_t(jnp.where(mine, gm, 0), v)
        gv = jnp.where(mine, dot_tn(probs.astype(bf16), gm), gv)
        row = jnp.sum(probs * gp, axis=-1, keepdims=True)
        gs = (probs * (gp - row)).astype(bf16)
        gq = jnp.where(mine, dot_n(gs, k), gq)
        gk = jnp.where(mine, dot_tn(gs, q), gk)
    gq = turn(gq * 0.125, first, cosine, -sine).astype(bf16)
    gk = turn(gk * 0.125, first, cosine, -sine).astype(bf16)
    gv = gv.astype(bf16)
    out_ref[:, :HC] = gq.astype(f32)
    out_ref[:, HC : 2 * HC] = gk.astype(f32)
    out_ref[:, 2 * HC :] = gv.astype(f32)

    @pl.when(pl.program_id(0) == 0)
    def _():
        bias_ref[...] = jnp.zeros_like(bias_ref)

    for i, g in enumerate((gq, gk, gv)):
        bias_ref[:, i * HC : (i + 1) * HC] += jnp.sum(g.astype(f32), axis=0, keepdims=True)


def group_specs():
    rows = lambda width: pl.BlockSpec((GR, width), lambda g: (g, 0))
    return dict(
        wide=rows(3 * HC),
        narrow=rows(HC),
        cols=rows(2),
        keys=pl.BlockSpec((None, 2, GR), lambda g: (g, 0, 0)),
        bias=pl.BlockSpec((1, 3 * HC), lambda g: (0, 0)),
    )


def attention(projected, bias, cosine, sine, colq, rowk):
    s = group_specs()
    n = projected.shape[0]
    return pl.pallas_call(
        attend_kernel,
        grid=(n // GR,),
        in_specs=[s["wide"], s["bias"], s["narrow"], s["narrow"], s["cols"], s["keys"]],
        out_specs=[s["wide"], s["narrow"]],
        out_shape=[jax.ShapeDtypeStruct((n, 3 * HC), f32), jax.ShapeDtypeStruct((n, HC), f32)],
        compiler_params=pltpu.CompilerParams(vmem_limit_bytes=32 << 20),
        cost_estimate=pl.CostEstimate(flops=4 * n * GR * HC * LH, bytes_accessed=n * HC * 28, transcendentals=n * GR * LH),
        name="attention",
    )(projected, bias, cosine, sine, colq, rowk)


def attention_back(qkv, grad, cosine, sine, colq, rowk):
    s = group_specs()
    n = qkv.shape[0]
    return pl.pallas_call(
        attend_back_kernel,
        grid=(n // GR,),
        in_specs=[s["wide"], s["narrow"], s["narrow"], s["narrow"], s["cols"], s["keys"]],
        out_specs=[s["wide"], s["bias"]],
        out_shape=[jax.ShapeDtypeStruct((n, 3 * HC), f32), jax.ShapeDtypeStruct((1, 3 * HC), f32)],
        compiler_params=pltpu.CompilerParams(vmem_limit_bytes=32 << 20),
        cost_estimate=pl.CostEstimate(flops=10 * n * GR * HC * LH, bytes_accessed=n * HC * 24, transcendentals=n * GR * LH),
        name="attention_back",
    )(qkv, grad, cosine, sine, colq, rowk)


def mm(spec, a, b):
    return jnp.einsum(spec, a, b, preferred_element_type=f32)


def pair_of(own, axis):
    other = send(own, **{axis: 1})
    first = lax.axis_index(axis) == 0
    return jnp.stack([jnp.where(first, own, other), jnp.where(first, other, own)])


def on_device(
    layer_in,
    segment,
    position,
    first_gain,
    first_shift,
    attend_weight,
    attend_bias,
    output_weight,
    second_gain,
    second_shift,
    gate_weight,
    up_weight,
    down_weight,
    cotangent,
):
    place = Place()
    own_block = place.block(0, 0)
    own_rows = lambda a: lax.dynamic_index_in_dim(a.reshape((NT, TOK) + a.shape[1:]), own_block, keepdims=False)

    joined = attend_weight.reshape(ROWS, 3, NT, HC).transpose(2, 0, 1, 3).reshape(NT, ROWS, 3 * HC)
    small = jnp.concatenate(
        [v.reshape(ROWS, 1) for v in (first_gain, first_shift, second_gain, second_shift)]
        + [attend_bias.reshape(ROWS, 3), jnp.zeros((ROWS, EXTRA - 7), bf16)],
        axis=1,
    )
    joined = jnp.concatenate([joined, jnp.broadcast_to(small[None], (NT, ROWS, EXTRA))], axis=2)
    joined = lax.all_to_all(joined, YC, 0, 0, tiled=True).reshape(NT * ROWS, 3 * HC + EXTRA)
    pairs = [(xz * NC + cc, (8 * cc + xz // 2) * NC + xz % 2) for xz in range(NXZ) for cc in range(NC)]
    out_own = lax.ppermute(to_pi(output_weight), ("x", "z", "c"), [(b, a) for a, b in pairs])
    out_own = out_own.reshape(ROWS, NT, HC).transpose(1, 0, 2).reshape(NT * ROWS, HC)
    first_own = jnp.concatenate([joined, out_own], axis=1)

    layer_pi = to_pi(layer_in[0])
    tokens = gather_rows(layer_pi, place)
    cot = to_pi(cotangent[0])
    here = jnp.concatenate([segment, position], axis=0).astype(f32)
    rowk = pair_of(here, "yl")
    rowk = pair_of(rowk, "c").transpose(1, 0, 2, 3).reshape(4, 2, GR)
    colq = rowk.transpose(0, 2, 1).reshape(NT * TOK, 2)
    _, cosine, sine = lane_tables(colq[:, 1:2])

    first_w = lax.all_gather(first_own, XZ, axis=0)
    hold = (tokens, gate_weight, up_weight, down_weight)
    tokens, gate_weight, up_weight, down_weight = lax.optimization_barrier(hold)

    spread = np.zeros((NXZ, FROWS, NXZ, FPAD), np.float32)
    for k in range(NXZ):
        spread[k, :, k, :FROWS] = np.eye(FROWS)
    spread = jnp.asarray(spread.reshape(NXZ * FROWS, FT), bf16)

    def hidden_cols(w):
        w = plain(w).reshape(ROWS, NT, NXZ * FROWS).transpose(1, 0, 2)
        return mm("trf,fg->trg", w, spread).astype(bf16)

    gate_up = jnp.concatenate([hidden_cols(gate_weight), hidden_cols(up_weight)], axis=2)
    gate_up = lax.all_to_all(gate_up, YC, 0, 0, tiled=True).reshape(NT * ROWS, 2 * FT)
    down_own = lax.ppermute(plain(down_weight), ("x", "z", "c"), [(b, a) for a, b in pairs])
    down_own = jnp.pad(to_pi(down_own), ((0, FPAD - FROWS), (0, 0)))

    def pack_down(a):
        rest = jnp.concatenate([a[..., 16 * i : 16 * i + 16, 2 * FT :] for i in range(3)], axis=-1)
        return jnp.concatenate([a[..., : 2 * FT], rest], axis=-2)

    def unpack_down(a):
        w = D - 2 * FT
        rest = jnp.concatenate([a[..., FPAD:, w * i : w * i + w] for i in range(3)], axis=-2)
        return jnp.concatenate([a[..., :FPAD, :], rest], axis=-1)

    second_own = jnp.concatenate([gate_up, pack_down(down_own)], axis=0)
    second_w = lax.all_gather(second_own, XZ, axis=0)
    gate_up_w = second_w[:, : NT * ROWS].reshape(D, 2 * FT)
    down_w = unpack_down(second_w[:, NT * ROWS :]).reshape(FT, D)

    cot_later, first_w = lax.optimization_barrier((cot, first_w))
    out_w = first_w[:, :, 3 * HC + EXTRA :].reshape(NXZ, NT, ROWS, HC).transpose(0, 2, 1, 3).reshape(HC, D)
    first_w = first_w[:, :, : 3 * HC + EXTRA].reshape(D, 3 * HC + EXTRA)
    joined_w = first_w[:, : 3 * HC]
    small_all = first_w[:, 3 * HC : 3 * HC + 8]
    vectors = small_all[:, :4].astype(f32).T
    gain_one, shift_one, gain_two, shift_two = (vectors[i : i + 1] for i in range(4))
    bias_all = small_all[:, 4:7].reshape(NXZ, NY, NC * ROWS * 3).transpose(1, 0, 2).reshape(3, NT, HC)
    bias = lax.dynamic_index_in_dim(bias_all, place.tensor(0, 0), axis=1, keepdims=False)
    bias = bias.reshape(1, 3 * HC).astype(f32)

    tokens_f = tokens.astype(f32)
    mean_one, inv_one = norm_stats(tokens_f)
    hidden1 = ((tokens_f - mean_one) * inv_one * gain_one + shift_one).astype(bf16)
    projected = mm("td,de->te", hidden1, joined_w)
    run = lambda projected: attention(projected, bias, cosine, sine, colq, rowk)
    grad_top, (qkv, mixed) = gather_rows(cot_later, place, (projected,), run)
    mixed = mixed.astype(bf16)
    attended = mm("td,de->te", mixed, out_w).astype(bf16)
    resid = layer_pi.astype(f32) + reduce_y(attended, place)

    mean_two, inv_two = norm_stats(resid)
    normed2 = (resid - mean_two) * inv_two
    hidden2 = (normed2 * gain_two + shift_two).astype(bf16)
    hidden2, (gate_up_w, down_w) = gather_rows(hidden2, place, (gate_up_w, down_w))
    gate_up_val = mm("td,de->te", hidden2, gate_up_w)
    gate_val, up_val = gate_up_val[:, :FT], gate_up_val[:, FT:]
    sig = jax.nn.sigmoid(gate_val)
    activated = gate_val * sig
    product = (activated * up_val).astype(bf16)

    grad_prod = mm("td,fd->tf", grad_top, down_w)
    grad_gate = (grad_prod * up_val * sig * (1.0 + gate_val * (1.0 - sig))).astype(bf16)
    grad_up = (grad_prod * activated).astype(bf16)
    grad_gu = jnp.concatenate([grad_gate, grad_up], axis=1)
    h2_part = mm("tf,df->td", grad_gu, gate_up_w)
    later = (product, grad_top, hidden2, grad_gu)
    grad_h2, (product, grad_top, hidden2, grad_gu) = reduce_y(h2_part.astype(bf16), place, later)

    down_grad = mm("tf,td->fd", product, grad_top)
    gate_up_grad = mm("td,tf->df", hidden2, grad_gu)
    second_chunks = jnp.concatenate(
        [gate_up_grad.astype(bf16).reshape(NXZ, NT * ROWS, 2 * FT), pack_down(down_grad.astype(bf16).reshape(NXZ, FPAD, D))],
        axis=1,
    )
    grad_h2, second_chunks = lax.optimization_barrier((grad_h2, second_chunks))
    gain_two_part = jnp.sum(grad_h2 * normed2, axis=0)
    shift_two_part = jnp.sum(grad_h2, axis=0)
    grad_resid = cot.astype(f32) + norm_back(grad_h2, normed2, inv_two, gain_two)
    second_sum = lax.psum_scatter(second_chunks.reshape(-1, 2 * FT), XZ, scatter_dimension=0, tiled=True)
    grad_branch = grad_resid.astype(bf16)
    branch_all = gather_rows(grad_branch, place)
    grad_mixed = mm("te,de->td", branch_all, out_w)
    grad_proj, bias_part = attention_back(qkv, grad_mixed, cosine, sine, colq, rowk)
    grad_proj, mixed, branch_all = lax.optimization_barrier((grad_proj.astype(bf16), mixed, branch_all))
    h1_part = mm("te,de->td", grad_proj, joined_w)
    normed1 = (tokens_f - mean_one) * inv_one
    gain_one_part = jnp.sum(h1_part * normed1, axis=0)
    shift_one_part = jnp.sum(h1_part, axis=0)
    out_grad = mm("td,te->de", mixed, branch_all).astype(bf16).reshape(NXZ, ROWS, D)
    joined_grad = mm("td,te->de", hidden1, grad_proj)
    bias_block = jnp.broadcast_to(bias_part.reshape(1, ROWS, 3 * HC // ROWS), (D // ROWS, ROWS, 3 * HC // ROWS))
    extra = jnp.concatenate(
        [
            gain_one_part[:, None],
            shift_one_part[:, None],
            gain_two_part[:, None],
            shift_two_part[:, None],
            bias_block.reshape(D, 3 * HC // ROWS),
            jnp.zeros((D, EXTRA - 4 - 3 * HC // ROWS), f32),
        ],
        axis=1,
    )
    blocks = lambda a: a.astype(bf16).reshape(NXZ, NT * ROWS, a.shape[-1])
    out_chunks = out_grad.reshape(NXZ, ROWS, NT, HC).transpose(0, 2, 1, 3).reshape(NXZ, NT * ROWS, HC)
    extra = lax.optimization_barrier(blocks(extra))
    first_chunks = jnp.concatenate([blocks(joined_grad), extra, out_chunks], axis=2)
    hold = (first_chunks, second_sum, h1_part.astype(bf16), product)
    first_chunks, second_sum, h1_part, product = lax.optimization_barrier(hold)
    first_sum = lax.psum_scatter(first_chunks.reshape(D, -1), XZ, scatter_dimension=0, tiled=True)
    grad_h1 = reduce_y(h1_part, place)
    out_part = mm("tf,fd->td", product, down_w).astype(bf16)
    layer_out = from_pi((resid + reduce_y(out_part, place)).astype(bf16))[None]
    input_grad = grad_resid + norm_back(grad_h1, own_rows(normed1), own_rows(inv_one), gain_one)
    input_grad = from_pi(input_grad.astype(bf16))[None]

    first_sum, layer_out, input_grad = lax.optimization_barrier((first_sum, layer_out, input_grad))
    down_sum = unpack_down(second_sum[NT * ROWS :])[:FROWS]
    down_sum = from_pi(lax.ppermute(plain(down_sum), ("x", "z", "c"), pairs)).astype(f32)
    gate_up_sum = second_sum[: NT * ROWS].reshape(NT, ROWS, 2 * FT)
    gate_up_sum = lax.all_to_all(gate_up_sum, YC, 0, 0, tiled=True)

    def weight_cols(a):
        a = mm("trg,fg->trf", a, spread)
        return a.transpose(1, 0, 2).reshape(ROWS, FF)

    gate_sum = weight_cols(gate_up_sum[:, :, :FT])
    up_sum = weight_cols(gate_up_sum[:, :, FT:])

    out_mine = first_sum[:, 3 * HC + EXTRA : 4 * HC + EXTRA].reshape(NT, ROWS, HC).transpose(1, 0, 2).reshape(ROWS, D)
    out_sum = from_pi(lax.ppermute(out_mine, ("x", "z", "c"), pairs)).astype(f32)
    joined_sum = first_sum[:, : 3 * HC + EXTRA].reshape(NT, ROWS, 3 * HC + EXTRA)
    joined_sum = lax.all_to_all(joined_sum, YC, 0, 0, tiled=True).astype(f32)
    attend_sum = joined_sum[:, :, : 3 * HC].reshape(NT, ROWS, 3, HC).transpose(1, 2, 0, 3).reshape(ROWS, 3 * D)
    summed = jnp.sum(joined_sum[:, :, 3 * HC : 3 * HC + 4], axis=0)
    gain_one_grad, shift_one_grad, gain_two_grad, shift_two_grad = (summed[:, i] for i in range(4))
    bias_sum = joined_sum[:, :, 3 * HC + 4 : 3 * HC + 4 + 3 * HC // ROWS].reshape(NT, 3, HC)
    bias_sum = bias_sum.transpose(1, 0, 2).reshape(3 * D)
    bias_grad = lax.dynamic_slice_in_dim(bias_sum, place.whole() * (3 * D // 128), 3 * D // 128)

    return (
        layer_out,
        input_grad,
        gain_one_grad,
        shift_one_grad,
        attend_sum,
        bias_grad,
        out_sum,
        gain_two_grad,
        shift_two_grad,
        gate_sum,
        up_sum,
        down_sum,
    )


def solution(mesh):
    fine = Mesh(np.asarray(mesh.devices).reshape([SIZES[a] for a in AXES]), AXES)
    group, every = ("yl", "x", "z", "c"), AXES
    tokens, whole = P(group, "yh", None), P(every)
    rows = P(every, None)
    return jax.shard_map(
        on_device,
        mesh=fine,
        in_specs=(
            tokens,
            P(group, None),
            P(group, None),
            whole,
            whole,
            rows,
            whole,
            rows,
            whole,
            whole,
            rows,
            rows,
            rows,
            tokens,
        ),
        out_specs=(tokens, tokens, whole, whole, rows, whole, rows, whole, whole, rows, rows, rows),
        check_vma=False,
    )
```

```python
import functools
import math

import jax
import jax.numpy as jnp
import numpy as np
from jax import lax
from jax.experimental import pallas as pl
from jax.experimental.pallas import tpu as pltpu
from jax.experimental.layout import Layout, with_layout_constraint
from jax.sharding import Mesh, PartitionSpec as P

HEADS = 32
HD = 64
D = 2048
FF = 5632
ROT = 16
EPS = 1e-05
TOK = 128
NY, NC, NX, NZ = 4, 2, 4, 4
NT = NY * NC
NXZ = NX * NZ
ROWS = D // (NT * NXZ)
FROWS = FF // (NT * NXZ)
FPAD = 48
FT = FPAD * NXZ
HC = D // NT
LH = HC // HD
EXTRA = 128
SIZES = {"yh": 2, "yl": 2, "x": NX, "z": NZ, "c": NC}
AXES = ("yh", "yl", "x", "z", "c")
YC = ("yh", "yl", "c")
XZ = ("x", "z")

f32 = jnp.float32
bf16 = jnp.bfloat16


def shift_perm(axes, deltas):
    sizes = [SIZES[a] for a in axes]
    pairs = []
    for src in range(math.prod(sizes)):
        coord = dict(zip(axes, np.unravel_index(src, sizes)))
        for key, delta in deltas.items():
            if key == "y":
                y = (2 * coord["yh"] + coord["yl"] + delta) % NY
                coord["yh"], coord["yl"] = y // 2, y % 2
            else:
                coord[key] = (coord[key] + delta) % SIZES[key]
        pairs.append((src, int(np.ravel_multi_index([coord[a] for a in axes], sizes))))
    return pairs


def plain(value):
    return with_layout_constraint(value, Layout(major_to_minor=tuple(range(value.ndim))))


def send(value, **deltas):
    axes = tuple(a for a in AXES if a in deltas or (a in ("yh", "yl") and "y" in deltas))
    return plain(lax.ppermute(plain(value), axes, shift_perm(axes, deltas)))


class Place:
    def __init__(self):
        yh, yl = lax.axis_index("yh"), lax.axis_index("yl")
        self.c, self.x, self.z = (lax.axis_index(a) for a in ("c", "x", "z"))
        self.y = 2 * yh + yl

    def tensor(self, ry, rc):
        return (self.y + ry) % NY * NC + (self.c ^ rc)

    def block(self, ry, rc):
        y = (self.y + ry) % NY
        return (y % 2 * NC + (self.c ^ rc)) * 2 + y // 2

    def whole(self):
        return ((self.y * NX + self.x) * NZ + self.z) * NC + self.c


EVERY = tuple((r, k) for r in range(NY) for k in range(NC))


def gather_y(own, half, hold, late=None):
    from_prev = send(own, y=1)
    from_next = send(own, y=-1)
    from_prev, from_next, hold = lax.optimization_barrier((from_prev, from_next, hold))
    top = send(from_prev[:half], y=1)
    bottom = send(from_next[half:], y=-1)
    if late:
        top, bottom, hold = lax.optimization_barrier((top, bottom, late(*hold)))
    blocks = {(0, 0): (own,), (1, 0): (from_next,), (3, 0): (from_prev,), (2, 0): (top, bottom)}
    for r in (0, 1, 3, 2):
        blocks[(r, 1)] = tuple(send(b, c=1) for b in blocks[(r, 0)])
    return blocks, hold


def gather_rows(own, place, hold=(), late=None):
    blocks, hold = gather_y(own, TOK // 2, hold, late)
    whole = jnp.zeros((NT,) + own.shape, own.dtype)
    for s in EVERY:
        at = 0
        for b in blocks[s]:
            whole = lax.dynamic_update_slice(whole, b[None], (place.block(*s), at, 0))
            at += b.shape[0]
    whole = whole.reshape(NT * TOK, own.shape[1])
    return (whole, hold) if hold else whole


def reduce_y(total, place, hold=()):
    total = total.reshape(NT, TOK, D)
    part = lambda r, k: lax.dynamic_index_in_dim(total, place.block(r, k), keepdims=False)
    sums = {r: part(r, 0).astype(f32) + send(part(r, 1), c=1).astype(f32) for r in (2, 1, 3, 0)}
    away, hold = lax.optimization_barrier(({r: sums[r].astype(bf16) for r in (2, 1, 3)}, hold))
    out = sums[0]
    for r in (2, 1, 3):
        out = out + send(away[r], y=r).astype(f32)
    return (out, hold) if hold else out


def reduce_y_steps(total, place, hold=()):
    total = total.reshape(NT, TOK, D)
    part = lambda r, k: lax.dynamic_index_in_dim(total, place.block(r, k), keepdims=False)
    sums = {}
    half = TOK // 2
    for r in (2, 1, 3, 0):
        other = send(part(r, 1), c=1)
        sums[r] = part(r, 0).astype(f32) + other.astype(f32)
    far, hold = lax.optimization_barrier((sums[2].astype(bf16), hold))
    top = send(far[:half], y=1)
    bottom = send(far[half:], y=-1)
    one = jnp.concatenate([sums[1][:half] + top.astype(f32), sums[1][half:]], axis=0).astype(bf16)
    three = jnp.concatenate([sums[3][:half], sums[3][half:] + bottom.astype(f32)], axis=0).astype(bf16)
    from_prev = send(one, y=1)
    from_next = send(three, y=-1)
    out = sums[0] + from_prev.astype(f32) + from_next.astype(f32)
    return (out, hold) if hold else out


def to_pi(a):
    n = a.shape[0]
    return plain(plain(a).reshape(n, NY, NXZ, D // NY // NXZ).transpose(0, 2, 1, 3).reshape(n, D))


def from_pi(a):
    n = a.shape[0]
    return plain(plain(a).reshape(n, NXZ, NY, D // NY // NXZ).transpose(0, 2, 1, 3).reshape(n, D))


def norm_stats(rows):
    mean = jnp.mean(rows, axis=-1, keepdims=True)
    centred = rows - mean
    var = jnp.mean(centred * centred, axis=-1, keepdims=True)
    return mean, lax.rsqrt(var + EPS)


def norm_back(grad_h, normed, inv_std, gain):
    grad_n = grad_h * gain
    return inv_std * (
        grad_n
        - jnp.mean(grad_n, axis=-1, keepdims=True)
        - normed * jnp.mean(grad_n * normed, axis=-1, keepdims=True)
    )


GR = 256


def lane_tables(pos):
    lane = lax.broadcasted_iota(jnp.int32, (1, HC), 1) % HD
    index = (lane % (ROT // 2)).astype(f32)
    freq = jnp.exp(index * (-2.0 * math.log(10000.0) / ROT))
    angles = pos * freq
    turned = lane < ROT
    cosine = jnp.where(turned, jnp.cos(angles), 1.0)
    sine = jnp.where(turned, jnp.sin(angles), 0.0)
    return lane < ROT // 2, cosine, sine


def turn(x, first, cosine, sine):
    ahead = pltpu.roll(x, HC - ROT // 2, 1)
    behind = pltpu.roll(x, ROT // 2, 1)
    return x * cosine + jnp.where(first, -ahead, behind) * sine


def dot_t(a, b):
    return lax.dot_general(a, b, (((1,), (1,)), ((), ())), preferred_element_type=f32)


def dot_n(a, b):
    return lax.dot_general(a, b, (((1,), (0,)), ((), ())), preferred_element_type=f32)


def dot_tn(a, b):
    return lax.dot_general(a, b, (((0,), (0,)), ((), ())), preferred_element_type=f32)


def readable(seg_q, pos_q, seg_k, pos_k):
    return (pos_k <= pos_q) & ((seg_k == 0.0) | (seg_k == seg_q))


def softmax_rows(scores):
    top = jnp.max(scores, axis=-1, keepdims=True)
    expo = jnp.exp(scores - top)
    return expo / jnp.sum(expo, axis=-1, keepdims=True)


def attend_kernel(proj_ref, bias_ref, cos_ref, sin_ref, colq_ref, rowk_ref, qkv_ref, mixed_ref):
    lane = lax.broadcasted_iota(jnp.int32, (1, HC), 1)
    first = (lane % HD) < ROT // 2
    cosine, sine = cos_ref[...], sin_ref[...]
    q = turn(proj_ref[:, :HC] + bias_ref[:, :HC], first, cosine, sine).astype(bf16)
    k = turn(proj_ref[:, HC : 2 * HC] + bias_ref[:, HC : 2 * HC], first, cosine, sine).astype(bf16)
    v = (proj_ref[:, 2 * HC :] + bias_ref[:, 2 * HC :]).astype(bf16)
    qkv_ref[:, :HC] = q.astype(f32)
    qkv_ref[:, HC : 2 * HC] = k.astype(f32)
    qkv_ref[:, 2 * HC :] = v.astype(f32)
    allowed = readable(colq_ref[:, 0:1], colq_ref[:, 1:2], rowk_ref[0:1, :], rowk_ref[1:2, :])
    out = jnp.zeros((GR, HC), f32)
    for h in range(LH):
        mine = (lane // HD) == h
        scores = dot_t(jnp.where(mine, q, 0), k) * 0.125
        probs = softmax_rows(jnp.where(allowed, scores, -1e30)).astype(bf16)
        out = jnp.where(mine, dot_n(probs, v), out)
    mixed_ref[...] = out


def attend_back_kernel(qkv_ref, grad_ref, cos_ref, sin_ref, colq_ref, rowk_ref, out_ref, bias_ref):
    lane = lax.broadcasted_iota(jnp.int32, (1, HC), 1)
    first = (lane % HD) < ROT // 2
    cosine, sine = cos_ref[...], sin_ref[...]
    q = qkv_ref[:, :HC].astype(bf16)
    k = qkv_ref[:, HC : 2 * HC].astype(bf16)
    v = qkv_ref[:, 2 * HC :].astype(bf16)
    gm = grad_ref[...].astype(bf16)
    allowed = readable(colq_ref[:, 0:1], colq_ref[:, 1:2], rowk_ref[0:1, :], rowk_ref[1:2, :])
    gq = jnp.zeros((GR, HC), f32)
    gk = jnp.zeros((GR, HC), f32)
    gv = jnp.zeros((GR, HC), f32)
    for h in range(LH):
        mine = (lane // HD) == h
        scores = dot_t(jnp.where(mine, q, 0), k) * 0.125
        probs = softmax_rows(jnp.where(allowed, scores, -1e30))
        gp = dot_t(jnp.where(mine, gm, 0), v)
        gv = jnp.where(mine, dot_tn(probs.astype(bf16), gm), gv)
        row = jnp.sum(probs * gp, axis=-1, keepdims=True)
        gs = (probs * (gp - row)).astype(bf16)
        gq = jnp.where(mine, dot_n(gs, k), gq)
        gk = jnp.where(mine, dot_tn(gs, q), gk)
    gq = turn(gq * 0.125, first, cosine, -sine).astype(bf16)
    gk = turn(gk * 0.125, first, cosine, -sine).astype(bf16)
    gv = gv.astype(bf16)
    out_ref[:, :HC] = gq.astype(f32)
    out_ref[:, HC : 2 * HC] = gk.astype(f32)
    out_ref[:, 2 * HC :] = gv.astype(f32)

    @pl.when(pl.program_id(0) == 0)
    def _():
        bias_ref[...] = jnp.zeros_like(bias_ref)

    for i, g in enumerate((gq, gk, gv)):
        bias_ref[:, i * HC : (i + 1) * HC] += jnp.sum(g.astype(f32), axis=0, keepdims=True)


def group_specs():
    rows = lambda width: pl.BlockSpec((GR, width), lambda g: (g, 0))
    return dict(
        wide=rows(3 * HC),
        narrow=rows(HC),
        cols=rows(2),
        keys=pl.BlockSpec((None, 2, GR), lambda g: (g, 0, 0)),
        bias=pl.BlockSpec((1, 3 * HC), lambda g: (0, 0)),
    )


def attention(projected, bias, cosine, sine, colq, rowk):
    s = group_specs()
    n = projected.shape[0]
    return pl.pallas_call(
        attend_kernel,
        grid=(n // GR,),
        in_specs=[s["wide"], s["bias"], s["narrow"], s["narrow"], s["cols"], s["keys"]],
        out_specs=[s["wide"], s["narrow"]],
        out_shape=[jax.ShapeDtypeStruct((n, 3 * HC), f32), jax.ShapeDtypeStruct((n, HC), f32)],
        compiler_params=pltpu.CompilerParams(vmem_limit_bytes=32 << 20),
        cost_estimate=pl.CostEstimate(flops=4 * n * GR * HC * LH, bytes_accessed=n * HC * 28, transcendentals=n * GR * LH),
        name="attention",
    )(projected, bias, cosine, sine, colq, rowk)


def attention_back(qkv, grad, cosine, sine, colq, rowk):
    s = group_specs()
    n = qkv.shape[0]
    return pl.pallas_call(
        attend_back_kernel,
        grid=(n // GR,),
        in_specs=[s["wide"], s["narrow"], s["narrow"], s["narrow"], s["cols"], s["keys"]],
        out_specs=[s["wide"], s["bias"]],
        out_shape=[jax.ShapeDtypeStruct((n, 3 * HC), f32), jax.ShapeDtypeStruct((1, 3 * HC), f32)],
        compiler_params=pltpu.CompilerParams(vmem_limit_bytes=32 << 20),
        cost_estimate=pl.CostEstimate(flops=10 * n * GR * HC * LH, bytes_accessed=n * HC * 24, transcendentals=n * GR * LH),
        name="attention_back",
    )(qkv, grad, cosine, sine, colq, rowk)


def mm(spec, a, b):
    return jnp.einsum(spec, a, b, preferred_element_type=f32)


def pair_of(own, axis):
    other = send(own, **{axis: 1})
    first = lax.axis_index(axis) == 0
    return jnp.stack([jnp.where(first, own, other), jnp.where(first, other, own)])


def on_device(
    layer_in,
    segment,
    position,
    first_gain,
    first_shift,
    attend_weight,
    attend_bias,
    output_weight,
    second_gain,
    second_shift,
    gate_weight,
    up_weight,
    down_weight,
    cotangent,
):
    place = Place()
    own_block = place.block(0, 0)
    own_rows = lambda a: lax.dynamic_index_in_dim(a.reshape((NT, TOK) + a.shape[1:]), own_block, keepdims=False)

    joined = attend_weight.reshape(ROWS, 3, NT, HC).transpose(2, 0, 1, 3).reshape(NT, ROWS, 3 * HC)
    small = jnp.concatenate(
        [v.reshape(ROWS, 1) for v in (first_gain, first_shift, second_gain, second_shift)]
        + [attend_bias.reshape(ROWS, 3), jnp.zeros((ROWS, EXTRA - 7), bf16)],
        axis=1,
    )
    joined = jnp.concatenate([joined, jnp.broadcast_to(small[None], (NT, ROWS, EXTRA))], axis=2)
    joined = lax.all_to_all(joined, YC, 0, 0, tiled=True).reshape(NT * ROWS, 3 * HC + EXTRA)
    pairs = [(xz * NC + cc, (8 * cc + xz // 2) * NC + xz % 2) for xz in range(NXZ) for cc in range(NC)]
    out_own = lax.ppermute(to_pi(output_weight), ("x", "z", "c"), [(b, a) for a, b in pairs])
    out_own = out_own.reshape(ROWS, NT, HC).transpose(1, 0, 2).reshape(NT * ROWS, HC)
    first_own = jnp.concatenate([joined, out_own], axis=1)

    layer_pi = to_pi(layer_in[0])
    tokens = gather_rows(layer_pi, place)
    cot = to_pi(cotangent[0])
    here = jnp.concatenate([segment, position], axis=0).astype(f32)
    rowk = pair_of(here, "yl")
    rowk = pair_of(rowk, "c").transpose(1, 0, 2, 3).reshape(4, 2, GR)
    colq = rowk.transpose(0, 2, 1).reshape(NT * TOK, 2)
    _, cosine, sine = lane_tables(colq[:, 1:2])

    first_w = lax.all_gather(first_own, XZ, axis=0)
    hold = (tokens, gate_weight, up_weight, down_weight)
    tokens, gate_weight, up_weight, down_weight = lax.optimization_barrier(hold)

    spread = np.zeros((NXZ, FROWS, NXZ, FPAD), np.float32)
    for k in range(NXZ):
        spread[k, :, k, :FROWS] = np.eye(FROWS)
    spread = jnp.asarray(spread.reshape(NXZ * FROWS, FT), bf16)

    def hidden_cols(w):
        w = plain(w).reshape(ROWS, NT, NXZ * FROWS).transpose(1, 0, 2)
        return mm("trf,fg->trg", w, spread).astype(bf16)

    gate_up = jnp.concatenate([hidden_cols(gate_weight), hidden_cols(up_weight)], axis=2)
    gate_up = lax.all_to_all(gate_up, YC, 0, 0, tiled=True).reshape(NT * ROWS, 2 * FT)
    down_own = lax.ppermute(plain(down_weight), ("x", "z", "c"), [(b, a) for a, b in pairs])
    down_own = jnp.pad(to_pi(down_own), ((0, FPAD - FROWS), (0, 0)))

    def pack_down(a):
        rest = jnp.concatenate([a[..., 16 * i : 16 * i + 16, 2 * FT :] for i in range(3)], axis=-1)
        return jnp.concatenate([a[..., : 2 * FT], rest], axis=-2)

    def unpack_down(a):
        w = D - 2 * FT
        rest = jnp.concatenate([a[..., FPAD:, w * i : w * i + w] for i in range(3)], axis=-2)
        return jnp.concatenate([a[..., :FPAD, :], rest], axis=-1)

    second_own = jnp.concatenate([gate_up, pack_down(down_own)], axis=0)
    second_w = lax.all_gather(second_own, XZ, axis=0)
    gate_up_w = second_w[:, : NT * ROWS].reshape(D, 2 * FT)
    down_w = unpack_down(second_w[:, NT * ROWS :]).reshape(FT, D)

    cot_later, first_w = lax.optimization_barrier((cot, first_w))
    out_w = first_w[:, :, 3 * HC + EXTRA :].reshape(NXZ, NT, ROWS, HC).transpose(0, 2, 1, 3).reshape(HC, D)
    first_w = first_w[:, :, : 3 * HC + EXTRA].reshape(D, 3 * HC + EXTRA)
    joined_w = first_w[:, : 3 * HC]
    small_all = first_w[:, 3 * HC : 3 * HC + 8]
    vectors = small_all[:, :4].astype(f32).T
    gain_one, shift_one, gain_two, shift_two = (vectors[i : i + 1] for i in range(4))
    bias_all = small_all[:, 4:7].reshape(NXZ, NY, NC * ROWS * 3).transpose(1, 0, 2).reshape(3, NT, HC)
    bias = lax.dynamic_index_in_dim(bias_all, place.tensor(0, 0), axis=1, keepdims=False)
    bias = bias.reshape(1, 3 * HC).astype(f32)

    tokens_f = tokens.astype(f32)
    mean_one, inv_one = norm_stats(tokens_f)
    hidden1 = ((tokens_f - mean_one) * inv_one * gain_one + shift_one).astype(bf16)
    projected = mm("td,de->te", hidden1, joined_w)
    run = lambda projected: attention(projected, bias, cosine, sine, colq, rowk)
    grad_top, (qkv, mixed) = gather_rows(cot_later, place, (projected,), run)
    mixed = mixed.astype(bf16)
    attended = mm("td,de->te", mixed, out_w).astype(bf16)
    resid = layer_pi.astype(f32) + reduce_y(attended, place)

    mean_two, inv_two = norm_stats(resid)
    normed2 = (resid - mean_two) * inv_two
    hidden2 = (normed2 * gain_two + shift_two).astype(bf16)
    hidden2, (gate_up_w, down_w) = gather_rows(hidden2, place, (gate_up_w, down_w))
    gate_up_val = mm("td,de->te", hidden2, gate_up_w)
    gate_val, up_val = gate_up_val[:, :FT], gate_up_val[:, FT:]
    sig = jax.nn.sigmoid(gate_val)
    activated = gate_val * sig
    product = (activated * up_val).astype(bf16)

    grad_prod = mm("td,fd->tf", grad_top, down_w)
    grad_gate = (grad_prod * up_val * sig * (1.0 + gate_val * (1.0 - sig))).astype(bf16)
    grad_up = (grad_prod * activated).astype(bf16)
    grad_gu = jnp.concatenate([grad_gate, grad_up], axis=1)
    h2_part = mm("tf,df->td", grad_gu, gate_up_w)
    later = (product, grad_top, hidden2, grad_gu)
    grad_h2, (product, grad_top, hidden2, grad_gu) = reduce_y(h2_part.astype(bf16), place, later)

    down_grad = mm("tf,td->fd", product, grad_top)
    gate_up_grad = mm("td,tf->df", hidden2, grad_gu)
    second_chunks = jnp.concatenate(
        [gate_up_grad.astype(bf16).reshape(NXZ, NT * ROWS, 2 * FT), pack_down(down_grad.astype(bf16).reshape(NXZ, FPAD, D))],
        axis=1,
    )
    grad_h2, second_chunks = lax.optimization_barrier((grad_h2, second_chunks))
    gain_two_part = jnp.sum(grad_h2 * normed2, axis=0)
    shift_two_part = jnp.sum(grad_h2, axis=0)
    grad_resid = cot.astype(f32) + norm_back(grad_h2, normed2, inv_two, gain_two)
    second_sum = lax.psum_scatter(second_chunks.reshape(-1, 2 * FT), XZ, scatter_dimension=0, tiled=True)
    grad_branch = grad_resid.astype(bf16)
    branch_all = gather_rows(grad_branch, place)
    grad_mixed = mm("te,de->td", branch_all, out_w)
    grad_proj, bias_part = attention_back(qkv, grad_mixed, cosine, sine, colq, rowk)
    grad_proj, mixed, branch_all = lax.optimization_barrier((grad_proj.astype(bf16), mixed, branch_all))
    h1_part = mm("te,de->td", grad_proj, joined_w)
    normed1 = (tokens_f - mean_one) * inv_one
    gain_one_part = jnp.sum(h1_part * normed1, axis=0)
    shift_one_part = jnp.sum(h1_part, axis=0)
    out_grad = mm("td,te->de", mixed, branch_all).astype(bf16).reshape(NXZ, ROWS, D)
    joined_grad = mm("td,te->de", hidden1, grad_proj)
    bias_block = jnp.broadcast_to(bias_part.reshape(1, ROWS, 3 * HC // ROWS), (D // ROWS, ROWS, 3 * HC // ROWS))
    extra = jnp.concatenate(
        [
            gain_one_part[:, None],
            shift_one_part[:, None],
            gain_two_part[:, None],
            shift_two_part[:, None],
            bias_block.reshape(D, 3 * HC // ROWS),
            jnp.zeros((D, EXTRA - 4 - 3 * HC // ROWS), f32),
        ],
        axis=1,
    )
    blocks = lambda a: a.astype(bf16).reshape(NXZ, NT * ROWS, a.shape[-1])
    out_chunks = out_grad.reshape(NXZ, ROWS, NT, HC).transpose(0, 2, 1, 3).reshape(NXZ, NT * ROWS, HC)
    extra = lax.optimization_barrier(blocks(extra))
    first_chunks = jnp.concatenate([blocks(joined_grad), extra, out_chunks], axis=2)
    hold = (first_chunks, second_sum, h1_part.astype(bf16), product)
    first_chunks, second_sum, h1_part, product = lax.optimization_barrier(hold)
    first_sum = lax.psum_scatter(first_chunks.reshape(D, -1), XZ, scatter_dimension=0, tiled=True)
    grad_h1 = reduce_y_steps(h1_part, place)
    out_part = mm("tf,fd->td", product, down_w).astype(bf16)
    layer_out = from_pi((resid + reduce_y_steps(out_part, place)).astype(bf16))[None]
    input_grad = grad_resid + norm_back(grad_h1, own_rows(normed1), own_rows(inv_one), gain_one)
    input_grad = from_pi(input_grad.astype(bf16))[None]

    first_sum, layer_out, input_grad = lax.optimization_barrier((first_sum, layer_out, input_grad))
    down_sum = unpack_down(second_sum[NT * ROWS :])[:FROWS]
    down_sum = from_pi(lax.ppermute(plain(down_sum), ("x", "z", "c"), pairs)).astype(f32)
    gate_up_sum = second_sum[: NT * ROWS].reshape(NT, ROWS, 2 * FT)
    gate_up_sum = lax.all_to_all(gate_up_sum, YC, 0, 0, tiled=True)

    def weight_cols(a):
        a = mm("trg,fg->trf", a, spread)
        return a.transpose(1, 0, 2).reshape(ROWS, FF)

    gate_sum = weight_cols(gate_up_sum[:, :, :FT])
    up_sum = weight_cols(gate_up_sum[:, :, FT:])

    out_mine = first_sum[:, 3 * HC + EXTRA : 4 * HC + EXTRA].reshape(NT, ROWS, HC).transpose(1, 0, 2).reshape(ROWS, D)
    out_sum = from_pi(lax.ppermute(out_mine, ("x", "z", "c"), pairs)).astype(f32)
    joined_sum = first_sum[:, : 3 * HC + EXTRA].reshape(NT, ROWS, 3 * HC + EXTRA)
    joined_sum = lax.all_to_all(joined_sum, YC, 0, 0, tiled=True).astype(f32)
    attend_sum = joined_sum[:, :, : 3 * HC].reshape(NT, ROWS, 3, HC).transpose(1, 2, 0, 3).reshape(ROWS, 3 * D)
    summed = jnp.sum(joined_sum[:, :, 3 * HC : 3 * HC + 4], axis=0)
    gain_one_grad, shift_one_grad, gain_two_grad, shift_two_grad = (summed[:, i] for i in range(4))
    bias_sum = joined_sum[:, :, 3 * HC + 4 : 3 * HC + 4 + 3 * HC // ROWS].reshape(NT, 3, HC)
    bias_sum = bias_sum.transpose(1, 0, 2).reshape(3 * D)
    bias_grad = lax.dynamic_slice_in_dim(bias_sum, place.whole() * (3 * D // 128), 3 * D // 128)

    return (
        layer_out,
        input_grad,
        gain_one_grad,
        shift_one_grad,
        attend_sum,
        bias_grad,
        out_sum,
        gain_two_grad,
        shift_two_grad,
        gate_sum,
        up_sum,
        down_sum,
    )


def solution(mesh):
    fine = Mesh(np.asarray(mesh.devices).reshape([SIZES[a] for a in AXES]), AXES)
    group, every = ("yl", "x", "z", "c"), AXES
    tokens, whole = P(group, "yh", None), P(every)
    rows = P(every, None)
    return jax.shard_map(
        on_device,
        mesh=fine,
        in_specs=(
            tokens,
            P(group, None),
            P(group, None),
            whole,
            whole,
            rows,
            whole,
            rows,
            whole,
            whole,
            rows,
            rows,
            rows,
            tokens,
        ),
        out_specs=(tokens, tokens, whole, whole, rows, whole, rows, whole, whole, rows, rows, rows),
        check_vma=False,
    )
```
